256 devices in a mesh: src: 128 (over z, y, x), act: 2 (over core).
Axes of the slice: x: 4, y: 4, z: 8, core: 2. Of those that a mesh axis runs over, the one named last changes fastest.
Arguments:
- position: float32 [3, 262144], P(None, 'src'), may hold values from -3 to 3
- velocity: float32 [3, 262144], P(None, 'src'), may hold values from -3 to 3
- accel: float32 [3, 262144], P(None, 'src'), may hold values from -6 to 6
- jerk_old: float32 [3, 262144], P(None, 'src'), may hold values from -6 to 6
- masses: float32 [262144], P('src'), may hold values from 1.9073486e-06 to 1.5258789e-05
- phase: float32 [262144], P('src'), may hold values from 0.25 to 1
- levels: int32 [262144], P('src'), may hold values from 0 to 3
- active: int32 [16, 128], P('act'), may hold values from 0 to 262143, as said below
Outputs:
- new_position: float32 [3, 262144], P(None, 'src')
- new_velocity: float32 [3, 262144], P(None, 'src')
- new_accel: float32 [3, 262144], P(None, 'src')
- new_jerk: float32 [3, 262144], P(None, 'src')
- active_update: float32 [12, 2048], P(None, 'act')
The draws below stay inside these ranges and needn't reach their ends.
Inputs may be any that keep to these rules, and one draw needn't show every extreme that they name: The 2048 active indices are distinct star indices. At most 64 active indices fall among the 2048 stars held by one index of src, and exactly 64 do at some index in every draw.
All inputs are finite; a program needn't handle non-finite values.
Results may differ from the reference program's by a relative error of at most 0.0001.
Values sent between devices are 32-bit elements; how exact they have to be, the bound alone decides.
No kernel may reach another device: no remote copies, remote signals or barrier semaphores. Data moves between devices by JAX's collectives and lax.ppermute only.
A program may use at most 64 MiB of HBM per device.

```python
import math
import jax
import jax.numpy as jnp
from jax import lax

SOURCE_STARS = 2048
STAR_TOTAL = 262144
ACT = 2048
OWN_MOST = 64


def draw_active(key, part):
    key = jax.random.fold_in(key, 7)
    keys = jax.random.split(key, 5)
    owner_ranks = STAR_TOTAL // SOURCE_STARS
    mean_load = ACT // owner_ranks
    star_bodies = jnp.arange(STAR_TOTAL, dtype=jnp.int32)
    owner_of = star_bodies // SOURCE_STARS
    local_place = star_bodies % SOURCE_STARS
    rank_list = jnp.arange(owner_ranks, dtype=jnp.int32)
    window_shift = jax.random.randint(keys[0], (owner_ranks,), 0, SOURCE_STARS)
    window_shift = jnp.where(rank_list == 0, 0, jnp.where(rank_list == owner_ranks - 1, 1, window_shift))
    owner_cap = jax.random.randint(keys[1], (owner_ranks,), mean_load, OWN_MOST + 1)
    busiest = jax.random.randint(keys[2], (), 0, owner_ranks)
    owner_cap = jnp.where(rank_list == busiest, OWN_MOST, owner_cap)
    placed = (local_place + window_shift[owner_of]) % SOURCE_STARS
    eligible = placed < owner_cap[owner_of]
    base_offset = jax.random.randint(keys[3], (STAR_TOTAL,), 0, 256)
    extra_credit = jax.random.randint(keys[4], (owner_ranks,), 0, 3) * 128
    credit = base_offset + extra_credit[owner_of]
    credit = jnp.where(owner_of == busiest, 700, credit)
    ends = (star_bodies == 0) | (star_bodies == STAR_TOTAL - 1)
    credit = jnp.where(ends, 800, credit)
    score_value = jnp.where(eligible, credit * STAR_TOTAL + star_bodies, -1 - star_bodies)
    chosen = lax.top_k(score_value, ACT)[1]
    return chosen.astype(jnp.int32).reshape(ACT // 128, 128)


def plant(result, rng, least, high):
    spot = [jax.random.randint(jax.random.fold_in(rng, axis), (), 0, length) for axis, length in enumerate(result.shape)]
    widest = result.shape.index(max(result.shape))
    next_to = spot[:widest] + [(spot[widest] + 1) % result.shape[widest]] + spot[widest + 1:]
    return result.at[tuple(spot)].set(least).at[tuple(next_to)].set(high)


def shard_levels(stream_key, extent, pieces, low, largest):
    def one(dim, blocks):
        steps = jax.random.uniform(jax.random.fold_in(jax.random.fold_in(stream_key, 6), dim), (blocks,), jnp.float32, low / len(pieces), largest / len(pieces))
        return jnp.repeat(jnp.exp(steps), extent[dim] // blocks).reshape((-1,) + (1,) * (len(extent) - dim - 1))

    loudness = one(*pieces[0])
    for cut in pieces[1:]:
        loudness = loudness * one(*cut)
    return loudness


def noise(rng, dims, scale, most, pieces=(), kind=jnp.bfloat16):
    factor_of = shard_levels(rng, dims, pieces, -0.22, 0.18) if pieces else 1.0
    array = jax.random.normal(rng, dims, jnp.float32) * scale * factor_of
    return jnp.minimum(jnp.maximum(array, -most), most).astype(kind)


def setup_inputs(seed: int = 0) -> dict:
    key_of = jax.random.split(jax.random.key(seed), 9)
    position = noise(key_of[0], (3, STAR_TOTAL), 0.5, 3.0, ((1, 128),), jnp.float32)
    velocity = noise(key_of[1], (3, STAR_TOTAL), 0.5, 3.0, ((1, 128),), jnp.float32)
    accel = noise(key_of[2], (3, STAR_TOTAL), 1.0, 6.0, ((1, 128),), jnp.float32)
    jerk_old = noise(key_of[3], (3, STAR_TOTAL), 1.0, 6.0, ((1, 128),), jnp.float32)
    masses = jnp.clip(jnp.exp(math.log(1.52587890625e-05) - 2.0794415 * jax.random.uniform(key_of[4], (STAR_TOTAL,), jnp.float32) ** shard_levels(key_of[4], (STAR_TOTAL,), ((0, 128),), -0.2, 0.2)), 1.9073486328125e-06, 1.52587890625e-05)
    phase = jnp.clip(0.25 + 0.75 * jax.random.uniform(key_of[5], (STAR_TOTAL,), jnp.float32) ** shard_levels(key_of[5], (STAR_TOTAL,), ((0, 128),), -0.2, 0.2), 0.25, 1.0)
    levels = plant(jax.random.randint(key_of[6], (STAR_TOTAL,), 0, 4), jax.random.fold_in(key_of[6], 1), 0, 3).astype(jnp.int32)
    active = draw_active(jax.random.fold_in(key_of[8], 71), 0)
    return {"position": position, "velocity": velocity, "accel": accel, "jerk_old": jerk_old, "masses": masses, "phase": phase, "levels": levels, "active": active}


softening = 0.0025

def predict(position, velocity, accel, jerk_old, phase, levels):
    tau = phase * jnp.exp2(-levels.astype(jnp.float32))
    pred_x = position + tau * (velocity + tau * (accel * 0.5 + tau * (jerk_old / 6.0)))
    pred_v = velocity + tau * (accel + tau * (jerk_old * 0.5))
    return (pred_x, pred_v, tau)

def pair_forces(act_x, act_v, src_x, src_v, src_m, width):
    count = src_x.shape[1] // width
    blocks_x = jnp.transpose(src_x.reshape(3, count, width), (1, 0, 2))
    blocks_v = jnp.transpose(src_v.reshape(3, count, width), (1, 0, 2))
    blocks_m = src_m.reshape(count, width)

    def step(carry, item):
        bx, bv, bm = item
        rel_x = bx[:, None, :] - act_x[:, :, None]
        rel_v = bv[:, None, :] - act_v[:, :, None]
        dist = lax.optimization_barrier(jnp.sum(rel_x * rel_x, axis=0)) + softening
        inv = lax.rsqrt(dist)
        weight = bm[None, :] * inv * inv * inv
        radial = 3.0 * lax.optimization_barrier(jnp.sum(rel_x * rel_v, axis=0)) / dist
        acc_add = lax.optimization_barrier(jnp.sum(weight[None] * rel_x, axis=2))
        jrk_add = lax.optimization_barrier(jnp.sum(weight[None] * (rel_v - radial[None] * rel_x), axis=2))
        return ((carry[0] + acc_add, carry[1] + jrk_add), None)
    zeros = jnp.zeros(act_x.shape, jnp.float32)
    totals, unused = lax.scan(step, (zeros, zeros), (blocks_x, blocks_v, blocks_m))
    return totals

def correct(state, acc_new, jrk_new):
    pred_x = state[0:3]
    pred_v = state[3:6]
    acc_old = state[6:9]
    jrk_old = state[9:12]
    step_dt = state[12:13]
    delta = acc_old - acc_new
    new_x = pred_x - step_dt * step_dt * (0.15 * delta + step_dt * (jrk_old * (7.0 / 60.0) + jrk_new / 30.0))
    new_v = pred_v - step_dt * (0.5 * delta + step_dt * (jrk_old * (5.0 / 12.0) + jrk_new / 12.0))
    return jnp.concatenate([new_x, new_v, acc_new, jrk_new], axis=0)

def reference(position, velocity, accel, jerk_old, masses, phase, levels, active):
    pred_x, pred_v, tau = predict(position, velocity, accel, jerk_old, phase, levels)
    index = active.reshape(-1).astype(jnp.int32)
    table = jnp.concatenate([pred_x, pred_v, accel, jerk_old, tau[None]], axis=0)
    state = jnp.take(table, index, axis=1)
    width = math.gcd(pred_x.shape[1], 1024)
    acc_new, jrk_new = pair_forces(state[0:3], state[3:6], pred_x, pred_v, masses, width)
    updated = correct(state, acc_new, jrk_new)
    new_position = position.at[:, index].set(updated[0:3])
    new_velocity = velocity.at[:, index].set(updated[3:6])
    new_accel = accel.at[:, index].set(updated[6:9])
    new_jerk = jerk_old.at[:, index].set(updated[9:12])
    return (new_position, new_velocity, new_accel, new_jerk, updated)
```

```python
import jax
import jax.numpy as jnp
from jax import lax
from jax.experimental import pallas as pl
from jax.experimental.pallas import tpu as pltpu
from jax.sharding import Mesh
from jax.sharding import PartitionSpec as P

softening = 0.0025
SLOTS = 64
LANES = 128
PLANE = ("y", "x")
SRC = ("z", "y", "x")
F32 = jnp.float32
BF16 = jnp.bfloat16
VMEM_LIMIT = 56 * 1024 * 1024


def params():
    return pltpu.CompilerParams(vmem_limit_bytes=VMEM_LIMIT)


def vmem():
    return pl.BlockSpec(memory_space=pltpu.VMEM)


def smem():
    return pl.BlockSpec(memory_space=pltpu.SMEM)


def three_terms(value):
    high = value.astype(BF16)
    rest = value - high.astype(F32)
    middle = rest.astype(BF16)
    low = (rest - middle.astype(F32)).astype(BF16)
    return high, middle, low


def iota(shape, axis):
    return lax.broadcasted_iota(jnp.int32, shape, axis)


def pick_kernel(me_ref, pos_ref, vel_ref, acc_ref, jrk_ref, mass_ref, phase_ref, level_ref, active_ref,
                send_ref, source_ref, place_ref):
    count = pos_ref.shape[1]
    rows = active_ref.shape[0]
    position, velocity = pos_ref[...], vel_ref[...]
    accel, jerk = acc_ref[...], jrk_ref[...]
    tau = phase_ref[...] * jnp.exp2(-level_ref[...].astype(F32))
    pred_x = position + tau * (velocity + tau * (accel * 0.5 + tau * (jerk / 6.0)))
    pred_v = velocity + tau * (accel + tau * (jerk * 0.5))
    base_x = pred_x - tau * tau * (0.15 * accel + tau * (jerk * (7.0 / 60.0)))
    base_v = pred_v - tau * (0.5 * accel + tau * (jerk * (5.0 / 12.0)))
    source_ref[...] = jnp.concatenate([pred_x, pred_v, mass_ref[...], tau], axis=0)

    offset = active_ref[...] - me_ref[0] * count
    owned = (offset >= 0) & (offset < count)
    flag = jnp.where(owned, 1.0, 0.0)
    before = jnp.where(iota((LANES, LANES), 0) < iota((LANES, LANES), 1), 1.0, 0.0)
    inside = jnp.dot(flag.astype(BF16), before.astype(BF16), preferred_element_type=F32)
    totals = jnp.sum(flag, axis=1, keepdims=True)
    running = jnp.zeros((1, 1), F32)
    place = jnp.zeros((SLOTS, LANES), jnp.int32)
    slot_id = iota((SLOTS, LANES), 0)
    for row in range(rows):
        slot = (inside[row:row + 1] + running).astype(jnp.int32)
        slot = jnp.where(owned[row:row + 1], slot, -1)
        place = place + jnp.where(slot_id == slot, offset[row:row + 1] + 1, 0)
        running = running + totals[row:row + 1]
    spot = jnp.sum(place.astype(F32), axis=1, keepdims=True).astype(jnp.int32) - 1
    place_ref[...] = jnp.broadcast_to(spot, (SLOTS, LANES))

    table = jnp.concatenate([pred_x, pred_v, tau, tau, base_x, base_v, tau, tau], axis=0)
    onehot = jnp.where(iota((SLOTS, count), 1) == spot, 1.0, 0.0).astype(BF16)
    picked = jnp.zeros((16, SLOTS), F32)
    for term in three_terms(table):
        picked = picked + lax.dot_general(term, onehot, (((1,), (1,)), ((), ())), preferred_element_type=F32)
    block = jnp.concatenate([picked[0:8], picked[8:16]], axis=1)
    send_ref[...] = jnp.broadcast_to(block[None], send_ref.shape)


def pick(me, position, velocity, accel, jerk_old, masses, phase, levels, active, owners):
    count = position.shape[1]
    return pl.pallas_call(
        pick_kernel,
        out_shape=(
            jax.ShapeDtypeStruct((owners, 8, LANES), F32),
            jax.ShapeDtypeStruct((8, count), F32),
            jax.ShapeDtypeStruct((SLOTS, LANES), jnp.int32),
        ),
        in_specs=[smem()] + [vmem()] * 8,
        out_specs=(vmem(), vmem(), vmem()),
        compiler_params=params(),
        name="pick",
    )(me, position, velocity, accel, jerk_old, masses, phase, levels, active)


def order_kernel(owners, source_ref, active_ref, mine_ref, other_ref, first_ref, perm_ref, onehot_ref, spread_ref):
    count = source_ref.shape[1]
    rows = active_ref.shape[0]
    total = rows * LANES
    active = active_ref[...]
    owner = lax.shift_right_logical(active, count.bit_length() - 1)
    key = (owner * total + iota((rows, LANES), 0) * LANES + iota((rows, LANES), 1)).astype(F32)
    columns = jnp.transpose(key)
    limit = (iota((1, LANES), 1) * total).astype(F32)
    first = jnp.zeros((8, LANES), F32)
    ranks = [jnp.zeros((8, LANES), F32) for _ in range(rows)]
    for row in range(rows):
        column = jnp.broadcast_to(columns[:, row:row + 1], (LANES, LANES))
        first = first + jnp.sum(jnp.where(column < limit, 1.0, 0.0).reshape(LANES // 8, 8, LANES), axis=0)
        for to in range(rows):
            less = jnp.where(column < key[to:to + 1], 1.0, 0.0)
            ranks[to] = ranks[to] + jnp.sum(less.reshape(LANES // 8, 8, LANES), axis=0)
    first_ref[...] = jnp.sum(first, axis=0, keepdims=True).astype(jnp.int32)
    spots = iota((total, LANES), 0)
    for to in range(rows):
        rank = jnp.sum(ranks[to], axis=0, keepdims=True).astype(jnp.int32)
        perm_ref[:, to * LANES:(to + 1) * LANES] = jnp.where(spots == rank, 1.0, 0.0).astype(BF16)
    lanes = iota((SLOTS, LANES), 1)
    for piece in range(count // LANES):
        here = slice(piece * LANES, (piece + 1) * LANES)
        onehot_ref[0:SLOTS, here] = jnp.where(mine_ref[...] == lanes + piece * LANES, 1.0, 0.0).astype(BF16)
        onehot_ref[SLOTS:2 * SLOTS, here] = jnp.where(other_ref[...] == lanes + piece * LANES, 1.0, 0.0).astype(BF16)
        across = jnp.transpose(source_ref[:, here])
        for field in range(7):
            spread_ref[field, here, :] = jnp.broadcast_to(across[:, field:field + 1], (LANES, LANES))


def order(source, active, mine, other, owners):
    count = source.shape[1]
    total = active.shape[0] * LANES
    return pl.pallas_call(
        lambda *refs: order_kernel(owners, *refs),
        out_shape=(
            jax.ShapeDtypeStruct((1, LANES), jnp.int32),
            jax.ShapeDtypeStruct((total, total), BF16),
            jax.ShapeDtypeStruct((2 * SLOTS, count), BF16),
            jax.ShapeDtypeStruct((7, count, LANES), F32),
        ),
        in_specs=[vmem()] * 4,
        out_specs=(vmem(), vmem(), vmem(), vmem()),
        compiler_params=params(),
        name="order",
    )(source, active, mine, other)


def force_kernel(first_ref, states_ref, spread_ref, send_ref, state_ref, compact):
    owners = states_ref.shape[0]
    count = spread_ref.shape[1]
    blocks = state_ref.shape[1]
    lane = iota((8, LANES), 1)

    def place(owner, unused):
        start = first_ref[0, owner]
        block = lax.shift_right_logical(start, 7)
        shift = lax.bitwise_and(start, LANES - 1)
        value = states_ref[owner]
        keep = lane >= shift
        for half in range(2):
            turned = pltpu.roll(value, lax.bitwise_and(shift + half * SLOTS, LANES - 1), 1)
            pltpu.store(compact.at[half, block], turned, mask=keep)
            compact[half, block + 1] = turned
        return unused

    lax.fori_loop(0, owners, place, 0, unroll=8)
    for field in range(16):
        state_ref[field] = compact[field // 8, 0:blocks, field % 8, :]

    width = 2
    for block in range(0, blocks, width):
        stars = [[jnp.broadcast_to(compact[0, block + b, f:f + 1, :], (8, LANES)) for f in range(6)] for b in range(width)]

        def step(group, sums):
            here = pl.ds(pl.multiple_of(group * 8, 8), 8)
            source = [spread_ref[f, here, :] for f in range(7)]
            result = []
            for b in range(width):
                star = stars[b]
                rx = [source[d] - star[d] for d in range(3)]
                rv = [source[3 + d] - star[3 + d] for d in range(3)]
                dist = rx[0] * rx[0] + rx[1] * rx[1] + (rx[2] * rx[2] + softening)
                inv = lax.rsqrt(dist)
                inv2 = inv * inv
                weight = source[6] * inv * inv2
                dot = rx[0] * rv[0] + rx[1] * rv[1] + rx[2] * rv[2]
                radial = weight * inv2 * dot
                old = sums[b]
                result.append(
                    tuple(old[d] + weight * rx[d] for d in range(3))
                    + tuple(old[3 + d] + weight * rv[d] for d in range(3))
                    + tuple(old[6 + d] + radial * rx[d] for d in range(3))
                )
            return tuple(result)

        zero = jnp.zeros((8, LANES), F32)
        sums = lax.fori_loop(0, count // 8, step, tuple((zero,) * 9 for _ in range(width)), unroll=2)
        for b in range(width):
            for d in range(3):
                acc = jnp.sum(sums[b][d], axis=0, keepdims=True)
                jrk = jnp.sum(sums[b][3 + d] - 3.0 * sums[b][6 + d], axis=0, keepdims=True)
                row = d * blocks + block + b
                send_ref[0, row:row + 1, :] = acc
                row = row + 3 * blocks
                send_ref[0, row:row + 1, :] = jrk
    for peer in range(1, send_ref.shape[0]):
        send_ref[peer] = send_ref[0]


def forces(first, states, spread, blocks, peers):
    return pl.pallas_call(
        force_kernel,
        out_shape=(
            jax.ShapeDtypeStruct((peers, 6 * blocks, LANES), F32),
            jax.ShapeDtypeStruct((16, blocks, LANES), F32),
        ),
        in_specs=[smem(), vmem(), vmem()],
        out_specs=(vmem(), vmem()),
        scratch_shapes=[pltpu.VMEM((2, blocks + 2, 8, LANES), F32)],
        compiler_params=params(),
        name="forces",
    )(first, states, spread)


def add_kernel(parts_ref, send_ref):
    total = jnp.sum(parts_ref[...], axis=0)
    send_ref[...] = jnp.broadcast_to(total[None], send_ref.shape)


def add_parts(parts, peers):
    return pl.pallas_call(
        add_kernel,
        out_shape=jax.ShapeDtypeStruct((peers,) + parts.shape[1:], F32),
        in_specs=[vmem()],
        out_specs=vmem(),
        compiler_params=params(),
        name="add_parts",
    )(parts)


def correct_kernel(me_ref, first_ref, parts_ref, state_ref, perm_ref, update_ref, own_ref, wide):
    blocks = state_ref.shape[1]
    total = jnp.sum(parts_ref[...], axis=0)
    tau = state_ref[6]
    t2 = tau * tau
    for d in range(3):
        acc = total[d * blocks:(d + 1) * blocks]
        jrk = total[(3 + d) * blocks:(4 + d) * blocks]
        wide[d, 0:blocks] = state_ref[8 + d] + t2 * (0.15 * acc - tau * (jrk / 30.0))
        wide[3 + d, 0:blocks] = state_ref[11 + d] + tau * (0.5 * acc - tau * (jrk / 12.0))
        wide[6 + d, 0:blocks] = acc
        wide[9 + d, 0:blocks] = jrk
    for f in range(12, 16):
        wide[f, 0:blocks] = jnp.ones_like(tau)
    wide[:, blocks:] = jnp.zeros((16, wide.shape[1] - blocks, LANES), F32)
    result = jnp.zeros((16, blocks * LANES), F32)
    for block in range(blocks):
        part = wide[:, block, :]
        rows = perm_ref[block * LANES:(block + 1) * LANES, :]
        for term in three_terms(part):
            result = result + jnp.dot(term, rows, preferred_element_type=F32)
    update_ref[...] = result[0:12]

    start = first_ref[0, me_ref[0]]
    block = lax.shift_right_logical(start, 7)
    shift = lax.bitwise_and(start, LANES - 1)
    back = lax.bitwise_and(LANES - shift, LANES - 1)
    lane = iota((16, LANES), 1)
    low = pltpu.roll(wide[:, block, :], back, 1)
    high = pltpu.roll(wide[:, block + 1, :], back, 1)
    own_ref[...] = jnp.where(lane < LANES - shift, low, high)


def correct(me, first, parts, state, perm):
    blocks = state.shape[1]
    return pl.pallas_call(
        correct_kernel,
        out_shape=(
            jax.ShapeDtypeStruct((12, blocks * LANES), F32),
            jax.ShapeDtypeStruct((16, LANES), F32),
        ),
        in_specs=[smem(), smem(), vmem(), vmem(), vmem()],
        out_specs=(vmem(), vmem()),
        scratch_shapes=[pltpu.VMEM((16, blocks + 2, LANES), F32)],
        compiler_params=params(),
        name="correct",
    )(me, first, parts, state, perm)


def write_kernel(mine_ref, other_ref, onehot_ref, pos_ref, vel_ref, acc_ref, jrk_ref,
                 new_pos_ref, new_vel_ref, new_acc_ref, new_jrk_ref):
    both = jnp.concatenate([mine_ref[:, 0:SLOTS], other_ref[:, 0:SLOTS]], axis=1)
    onehot = onehot_ref[...]
    values = jnp.zeros((16, onehot.shape[1]), F32)
    for term in three_terms(both):
        values = values + jnp.dot(term, onehot, preferred_element_type=F32)
    hit = values[12:13] > 0.5
    new_pos_ref[...] = jnp.where(hit, values[0:3], pos_ref[...])
    new_vel_ref[...] = jnp.where(hit, values[3:6], vel_ref[...])
    new_acc_ref[...] = jnp.where(hit, values[6:9], acc_ref[...])
    new_jrk_ref[...] = jnp.where(hit, values[9:12], jrk_ref[...])


def write(mine, other, onehot, position, velocity, accel, jerk_old):
    shape = jax.ShapeDtypeStruct(position.shape, F32)
    return pl.pallas_call(
        write_kernel,
        out_shape=(shape,) * 4,
        in_specs=[vmem()] * 7,
        out_specs=(vmem(),) * 4,
        compiler_params=params(),
        name="write",
    )(mine, other, onehot, position, velocity, accel, jerk_old)


def swap(value):
    return lax.ppermute(value, "core", [(0, 1), (1, 0)])


def exchange(value, axes):
    return lax.all_to_all(value, axes, 0, 0, tiled=True)


def local(owners, plane, depth, position, velocity, accel, jerk_old, masses, phase, levels, active):
    count = position.shape[1]
    blocks = active.shape[0]
    me = lax.axis_index(SRC).reshape(1).astype(jnp.int32)
    send, source, mine = pick(
        me, position, velocity, accel, jerk_old, masses.reshape(1, count), phase.reshape(1, count),
        levels.reshape(1, count), active, owners,
    )
    states = exchange(send, SRC)
    other = swap(mine)
    first, perm, onehot, spread = order(source, active, mine, other, owners)
    send, state = forces(first, states, spread, blocks, plane)
    send = add_parts(exchange(send, PLANE), depth)
    update, own = correct(me, first, exchange(send, "z"), state, perm)
    new = write(own, swap(own), onehot, position, velocity, accel, jerk_old)
    return new + (update,)


def solution(mesh):
    owners = mesh.shape["src"]
    plane = 16
    depth = owners // plane
    fine = Mesh(mesh.devices.reshape(depth, 4, 4, mesh.shape["act"]), ("z", "y", "x", "core"))
    stars = P(None, SRC)
    placed = (stars,) * 4 + (P(SRC),) * 3 + (P("core", None),)
    return jax.shard_map(
        lambda *arrays: local(owners, plane, depth, *arrays),
        mesh=fine,
        in_specs=placed,
        out_specs=(stars,) * 4 + (P(None, "core"),),
        check_vma=False,
    )
```

```python
import jax
import jax.numpy as jnp
from jax import lax
from jax.experimental import pallas as pl
from jax.experimental.pallas import tpu as pltpu
from jax.sharding import Mesh
from jax.sharding import PartitionSpec as P

softening = 0.0025
SLOTS = 64
LANES = 128
PLANE = ("y", "x")
SRC = ("z", "y", "x")
F32 = jnp.float32
BF16 = jnp.bfloat16
PREP = 56
PAIRS = ((0, 0), (0, 1), (1, 0), (1, 1), (0, 2), (2, 0))


def params(mebibytes):
    return pltpu.CompilerParams(vmem_limit_bytes=mebibytes << 20)


def cost(microseconds):
    return pl.CostEstimate(flops=0, transcendentals=0, bytes_accessed=microseconds * 3000000)


def vmem():
    return pl.BlockSpec(memory_space=pltpu.VMEM)


def hbm():
    return pl.BlockSpec(memory_space=pltpu.HBM)


def pinned(value):
    return pltpu.with_memory_space_constraint(value, pltpu.HBM)


def smem():
    return pl.BlockSpec(memory_space=pltpu.SMEM)


def three_terms(value):
    high = value.astype(BF16)
    rest = value - high.astype(F32)
    middle = rest.astype(BF16)
    low = (rest - middle.astype(F32)).astype(BF16)
    return high, middle, low


def iota(shape, axis):
    return lax.broadcasted_iota(jnp.int32, shape, axis)


def pick_kernel(me_ref, pos_ref, vel_ref, acc_ref, jrk_ref, mass_ref, phase_ref, level_ref, active_ref,
                send_ref, source_ref, place_ref):
    count = pos_ref.shape[1]
    rows = active_ref.shape[0]
    position, velocity = pos_ref[...], vel_ref[...]
    accel, jerk = acc_ref[...], jrk_ref[...]
    tau = phase_ref[...] * jnp.exp2(-level_ref[...].astype(F32))
    pred_x = position + tau * (velocity + tau * (accel * 0.5 + tau * (jerk / 6.0)))
    pred_v = velocity + tau * (accel + tau * (jerk * 0.5))
    base_x = pred_x - tau * tau * (0.15 * accel + tau * (jerk * (7.0 / 60.0)))
    base_v = pred_v - tau * (0.5 * accel + tau * (jerk * (5.0 / 12.0)))
    source_ref[...] = jnp.concatenate([pred_x, pred_v, mass_ref[...], tau], axis=0)

    offset = active_ref[...] - me_ref[0] * count
    owned = (offset >= 0) & (offset < count)
    flag = jnp.where(owned, 1.0, 0.0)
    before = jnp.where(iota((LANES, LANES), 0) < iota((LANES, LANES), 1), 1.0, 0.0)
    inside = jnp.dot(flag.astype(BF16), before.astype(BF16), preferred_element_type=F32)
    totals = jnp.sum(flag, axis=1, keepdims=True)
    running = jnp.zeros((1, 1), F32)
    place = jnp.zeros((SLOTS, LANES), jnp.int32)
    slot_id = iota((SLOTS, LANES), 0)
    for row in range(rows):
        slot = (inside[row:row + 1] + running).astype(jnp.int32)
        slot = jnp.where(owned[row:row + 1], slot, -1)
        place = place + jnp.where(slot_id == slot, offset[row:row + 1] + 1, 0)
        running = running + totals[row:row + 1]
    spot = jnp.sum(place.astype(F32), axis=1, keepdims=True).astype(jnp.int32) - 1
    place_ref[...] = jnp.broadcast_to(spot, (SLOTS, LANES))

    table = jnp.concatenate([pred_x, pred_v, tau, tau, base_x, base_v, tau, tau], axis=0)
    onehot = jnp.where(iota((SLOTS, count), 1) == spot, 1.0, 0.0).astype(BF16)
    terms = jnp.concatenate(three_terms(table), axis=0)
    picked = lax.dot_general(terms, onehot, (((1,), (1,)), ((), ())), preferred_element_type=F32)
    picked = picked[0:16] + picked[16:32] + picked[32:48]
    block = jnp.concatenate([picked[0:8], picked[8:16]], axis=1)
    send_ref[...] = jnp.broadcast_to(block[None], send_ref.shape)


def pick(me, position, velocity, accel, jerk_old, masses, phase, levels, active, owners):
    count = position.shape[1]
    return pl.pallas_call(
        pick_kernel,
        out_shape=(
            jax.ShapeDtypeStruct((owners, 8, LANES), F32),
            jax.ShapeDtypeStruct((8, count), F32),
            jax.ShapeDtypeStruct((SLOTS, LANES), jnp.int32),
        ),
        in_specs=[smem()] + [vmem()] * 8,
        out_specs=(vmem(), vmem(), vmem()),
        compiler_params=params(56),
        name="pick",
    )(me, position, velocity, accel, jerk_old, masses, phase, levels, active)


def sort_keys(active, count):
    rows = active.shape[0]
    owner = lax.shift_right_logical(active, count.bit_length() - 1)
    return (owner * (rows * LANES) + iota((rows, LANES), 0) * LANES + iota((rows, LANES), 1)).astype(F32)


def prepare_kernel(source_ref, active_ref, first_ref, factor_ref, moment_ref, spread_ref):
    count = source_ref.shape[1]
    rows = active_ref.shape[0]
    total = rows * LANES
    key = sort_keys(active_ref[...], count)
    columns = jnp.transpose(key)
    limit = (iota((1, LANES), 1) * total).astype(F32)
    first = jnp.zeros((8, LANES), F32)
    for row in range(rows):
        column = jnp.broadcast_to(columns[:, row:row + 1], (LANES, LANES))
        first = first + jnp.sum(jnp.where(column < limit, 1.0, 0.0).reshape(LANES // 8, 8, LANES), axis=0)
    first_ref[...] = jnp.sum(first, axis=0, keepdims=True).astype(jnp.int32)

    source = source_ref[...]
    terms = [term.astype(F32) for term in three_terms(source)]
    product = source[0:1] * source[3:4] + source[1:2] * source[4:5] + source[2:3] * source[5:6]
    product = [term.astype(F32) for term in three_terms(product)]
    one = jnp.ones((3, count), F32)
    last = jnp.concatenate(product + [one, jnp.zeros((2, count), F32)], axis=0)
    stack = jnp.concatenate([terms[a] for a, unused in PAIRS] + [last], axis=0)
    mass = source[6:7]
    moments = jnp.concatenate([mass * source[0:6], mass, jnp.zeros((1, count), F32)], axis=0)
    moments = [term.astype(F32) for term in three_terms(moments)]
    moment_ref[...] = jnp.concatenate(moments + [jnp.zeros((8, count), F32)], axis=0).astype(BF16)
    for piece in range(count // LANES):
        here = slice(piece * LANES, (piece + 1) * LANES)
        across = jnp.transpose(stack[:, here])
        factor_ref[here, :] = jnp.concatenate([across, jnp.zeros((LANES, LANES - 56), F32)], axis=1).astype(BF16)
        across = jnp.transpose(source[:, here])
        for field in range(3):
            spread_ref[field, here, :] = jnp.broadcast_to(across[:, field:field + 1], (LANES, LANES))


def prepare(source, active):
    count = source.shape[1]
    return pl.pallas_call(
        prepare_kernel,
        out_shape=(
            jax.ShapeDtypeStruct((1, LANES), jnp.int32),
            jax.ShapeDtypeStruct((count, LANES), BF16),
            jax.ShapeDtypeStruct((32, count), BF16),
            jax.ShapeDtypeStruct((3, count, LANES), F32),
        ),
        in_specs=[vmem()] * 2,
        out_specs=(vmem(),) * 4,
        compiler_params=params(PREP),
        cost_estimate=cost(5),
        name="prepare",
    )(source, active)


def place(first_ref, states_ref, compact, half, owner):
    start = first_ref[0, owner]
    block = lax.shift_right_logical(start, 7)
    shift = lax.bitwise_and(start, LANES - 1)
    turned = pltpu.roll(states_ref[owner], lax.bitwise_and(shift + half * SLOTS, LANES - 1), 1)
    pltpu.store(compact.at[block], turned, mask=iota((8, LANES), 1) >= shift)
    compact[block + 1] = turned


def tables_kernel(count, active_ref, perm_ref):
    rows = active_ref.shape[0]
    total = rows * LANES
    key = sort_keys(active_ref[...], count)
    columns = jnp.transpose(key)
    ranks = [jnp.zeros((8, LANES), F32) for _ in range(rows)]
    for row in range(rows):
        column = jnp.broadcast_to(columns[:, row:row + 1], (LANES, LANES))
        for to in range(rows):
            less = jnp.where(column < key[to:to + 1], 1.0, 0.0)
            ranks[to] = ranks[to] + jnp.sum(less.reshape(LANES // 8, 8, LANES), axis=0)
    spots = iota((total, LANES), 0)
    for to in range(rows):
        rank = jnp.sum(ranks[to], axis=0, keepdims=True).astype(jnp.int32)
        perm_ref[:, to * LANES:(to + 1) * LANES] = jnp.where(spots == rank, 1.0, 0.0).astype(BF16)


def tables(active, count):
    total = active.shape[0] * LANES
    return pl.pallas_call(
        lambda *refs: tables_kernel(count, *refs),
        out_shape=jax.ShapeDtypeStruct((total, total), BF16),
        in_specs=[vmem()],
        out_specs=vmem(),
        compiler_params=params(8),
        cost_estimate=cost(4),
        name="tables",
    )(active)


def force_kernel(first_hbm, states_ref, factor_hbm, moment_hbm, spread_hbm, send_ref, state_ref,
                 compact, later, first_ref, factor_ref, moment_ref, spread_ref, arrived):
    owners = states_ref.shape[0]
    count = spread_ref.shape[1]
    blocks = send_ref.shape[1] // 6
    pairs = ((first_hbm, first_ref), (factor_hbm, factor_ref), (moment_hbm, moment_ref), (spread_hbm, spread_ref))
    copies = [pltpu.make_async_copy(here, there, arrived.at[i]) for i, (here, there) in enumerate(pairs)]
    for copy in copies:
        copy.start()
    copies[0].wait()

    def place_early(owner, unused):
        place(first_ref, states_ref, compact, 0, owner)
        return unused

    lax.fori_loop(0, owners, place_early, 0, unroll=16)
    for copy in copies[1:]:
        copy.wait()
    wide, deep = 2, min(1024, count)
    width = wide * LANES

    def part(block):
        tiles = [compact[block + b] for b in range(wide)]
        star = jnp.concatenate(tiles, axis=1)
        x, v = star[0:3], star[3:6]
        swapped = jnp.concatenate([-v, -x, jnp.zeros((2, width), F32)], axis=0)
        terms = [term.astype(F32) for term in three_terms(swapped)]
        product = [term.astype(F32) for term in three_terms(x[0:1] * v[0:1] + x[1:2] * v[1:2] + x[2:3] * v[2:3])]
        last = jnp.concatenate([jnp.ones((3, width), F32)] + product + [jnp.zeros((2, width), F32)], axis=0)
        cross = jnp.concatenate(
            [terms[b] for unused, b in PAIRS] + [last, jnp.zeros((LANES - 56, width), F32)], axis=0
        ).astype(BF16)
        weighted = jnp.zeros((32, width), F32)
        radial = jnp.zeros((32, width), F32)
        for low in range(0, count, deep):
            here = slice(low, low + deep)
            rel = [jnp.concatenate([spread_ref[d, here, :]] * wide, axis=1) - x[d:d + 1] for d in range(3)]
            dist = rel[0] * rel[0] + rel[1] * rel[1] + (rel[2] * rel[2] + softening)
            inv = lax.rsqrt(dist)
            inv2 = inv * inv
            weight = inv * inv2
            dot = jnp.dot(factor_ref[here, :], cross, preferred_element_type=F32)
            turn = weight * inv2 * dot
            moment = moment_ref[:, here]
            weight_high, turn_high = weight.astype(BF16), turn.astype(BF16)
            weight_low = (weight - weight_high.astype(F32)).astype(BF16)
            turn_low = (turn - turn_high.astype(F32)).astype(BF16)
            weighted = weighted + jnp.dot(moment, weight_high, preferred_element_type=F32)
            weighted = weighted + jnp.dot(moment, weight_low, preferred_element_type=F32)
            radial = radial + jnp.dot(moment, turn_high, preferred_element_type=F32)
            radial = radial + jnp.dot(moment, turn_low, preferred_element_type=F32)
        weighted = weighted[0:8] + weighted[8:16] + weighted[16:24]
        radial = radial[0:8] + radial[8:16] + radial[16:24]
        acc = weighted[0:3] - x * weighted[6:7]
        jrk = weighted[3:6] - v * weighted[6:7] - 3.0 * (radial[0:3] - x * radial[6:7])
        for b in range(wide):
            for d in range(3):
                send_ref[0, pl.ds(d * blocks + block + b, 1), :] = acc[d:d + 1, b * LANES:(b + 1) * LANES]
                send_ref[0, pl.ds((3 + d) * blocks + block + b, 1), :] = jrk[d:d + 1, b * LANES:(b + 1) * LANES]

    def pair_of_parts(index, unused):
        part(index * (2 * wide))
        part(index * (2 * wide) + wide)
        for owner in range(owners // rounds):
            place(first_ref, states_ref, later, 1, index * (owners // rounds) + owner)
        return unused

    rounds = blocks // (2 * wide)
    lax.fori_loop(0, rounds, pair_of_parts, 0)
    for field in range(8):
        state_ref[field] = later[0:blocks, field, :]
    for peer in range(1, send_ref.shape[0]):
        send_ref[peer] = send_ref[0]


def forces(first, states, factor, moment, spread, blocks, peers):
    return pl.pallas_call(
        force_kernel,
        out_shape=(
            jax.ShapeDtypeStruct((peers, 6 * blocks, LANES), F32),
            jax.ShapeDtypeStruct((8, blocks, LANES), F32),
        ),
        in_specs=[hbm(), vmem(), hbm(), hbm(), hbm()],
        out_specs=(vmem(), vmem()),
        scratch_shapes=[
            pltpu.VMEM((blocks + 2, 8, LANES), F32),
            pltpu.VMEM((blocks + 2, 8, LANES), F32),
            pltpu.SMEM(first.shape, first.dtype),
            pltpu.VMEM(factor.shape, factor.dtype),
            pltpu.VMEM(moment.shape, moment.dtype),
            pltpu.VMEM(spread.shape, spread.dtype),
            pltpu.SemaphoreType.DMA((4,)),
        ],
        compiler_params=params(12),
        cost_estimate=cost(9),
        name="forces",
    )(pinned(first), states, pinned(factor), pinned(moment), pinned(spread))


def add_kernel(parts_ref, send_ref):
    total = jnp.sum(parts_ref[...], axis=0)
    send_ref[...] = jnp.broadcast_to(total[None], send_ref.shape)


def add_parts(parts, peers):
    return pl.pallas_call(
        add_kernel,
        out_shape=jax.ShapeDtypeStruct((peers,) + parts.shape[1:], F32),
        in_specs=[vmem()],
        out_specs=vmem(),
        compiler_params=params(4),
        name="add_parts",
    )(parts)


def correct_kernel(me_ref, first_ref, parts_ref, state_ref, own_ref, wide_ref):
    blocks = state_ref.shape[1]
    total = jnp.sum(parts_ref[...], axis=0)
    tau = state_ref[6]
    t2 = tau * tau
    for d in range(3):
        acc = total[d * blocks:(d + 1) * blocks]
        jrk = total[(3 + d) * blocks:(4 + d) * blocks]
        wide_ref[d, 0:blocks] = state_ref[d] + t2 * (0.15 * acc - tau * (jrk / 30.0))
        wide_ref[3 + d, 0:blocks] = state_ref[3 + d] + tau * (0.5 * acc - tau * (jrk / 12.0))
        wide_ref[6 + d, 0:blocks] = acc
        wide_ref[9 + d, 0:blocks] = jrk
    for f in range(12, 16):
        wide_ref[f, 0:blocks] = jnp.ones_like(tau)
    wide_ref[:, blocks:] = jnp.zeros((16, wide_ref.shape[1] - blocks, LANES), F32)
    start = first_ref[0, me_ref[0]]
    block = lax.shift_right_logical(start, 7)
    shift = lax.bitwise_and(start, LANES - 1)
    back = lax.bitwise_and(LANES - shift, LANES - 1)
    lane = iota((16, LANES), 1)
    low = pltpu.roll(wide_ref[:, block, :], back, 1)
    high = pltpu.roll(wide_ref[:, block + 1, :], back, 1)
    own_ref[...] = jnp.where(lane < LANES - shift, low, high)


def correct(me, first, parts, state):
    blocks = state.shape[1]
    return pl.pallas_call(
        correct_kernel,
        out_shape=(
            jax.ShapeDtypeStruct((16, LANES), F32),
            jax.ShapeDtypeStruct((16, blocks + 2, LANES), F32),
        ),
        in_specs=[smem(), smem(), vmem(), vmem()],
        out_specs=(vmem(), vmem()),
        compiler_params=params(4),
        name="correct",
    )(me, first, parts, state)


def permute_kernel(wide_ref, perm_ref, update_ref):
    blocks = perm_ref.shape[0] // LANES
    value = jnp.concatenate([wide_ref[:, block, :] for block in range(blocks)], axis=1)
    terms = jnp.concatenate(three_terms(value), axis=0)
    result = jnp.dot(terms, perm_ref[...], preferred_element_type=F32)
    update_ref[...] = (result[0:16] + result[16:32] + result[32:48])[0:12]


def permute(wide, perm):
    return pl.pallas_call(
        permute_kernel,
        out_shape=jax.ShapeDtypeStruct((12, perm.shape[1]), F32),
        in_specs=[vmem(), vmem()],
        out_specs=vmem(),
        compiler_params=params(8),
        cost_estimate=cost(2),
        name="permute",
    )(wide, perm)


def write_kernel(mine_ref, other_ref, here_ref, there_ref, pos_ref, vel_ref, acc_ref, jrk_ref,
                 new_pos_ref, new_vel_ref, new_acc_ref, new_jrk_ref):
    count = pos_ref.shape[1]
    both = jnp.concatenate([mine_ref[:, 0:SLOTS], other_ref[:, 0:SLOTS]], axis=1)
    place = jnp.concatenate([here_ref[...], there_ref[...]], axis=0)[:, 0:1]
    onehot = jnp.where(iota((2 * SLOTS, count), 1) == place, 1.0, 0.0).astype(BF16)
    values = jnp.dot(jnp.concatenate(three_terms(both), axis=0), onehot, preferred_element_type=F32)
    values = values[0:16] + values[16:32] + values[32:48]
    hit = values[12:13] > 0.5
    new_pos_ref[...] = jnp.where(hit, values[0:3], pos_ref[...])
    new_vel_ref[...] = jnp.where(hit, values[3:6], vel_ref[...])
    new_acc_ref[...] = jnp.where(hit, values[6:9], acc_ref[...])
    new_jrk_ref[...] = jnp.where(hit, values[9:12], jrk_ref[...])


def write(mine, other, here, there, position, velocity, accel, jerk_old):
    shape = jax.ShapeDtypeStruct(position.shape, F32)
    return pl.pallas_call(
        write_kernel,
        out_shape=(shape,) * 4,
        in_specs=[vmem()] * 8,
        out_specs=(vmem(),) * 4,
        compiler_params=params(4),
        name="write",
    )(mine, other, here, there, position, velocity, accel, jerk_old)


def swap(value):
    return lax.ppermute(value, "core", [(0, 1), (1, 0)])


def exchange(value, axes):
    return lax.all_to_all(value, axes, 0, 0, tiled=True)


def local(owners, plane, depth, position, velocity, accel, jerk_old, masses, phase, levels, active):
    count = position.shape[1]
    blocks = active.shape[0]
    me = lax.axis_index(SRC).reshape(1).astype(jnp.int32)
    send, source, mine = pick(
        me, position, velocity, accel, jerk_old, masses.reshape(1, count), phase.reshape(1, count),
        levels.reshape(1, count), active, owners,
    )
    states = exchange(send, SRC)
    other = swap(mine)
    first, factor, moment, spread = prepare(source, active)
    perm = tables(active, count)
    states, other, perm = lax.optimization_barrier((states, other, perm))
    send, state = forces(first, states, factor, moment, spread, blocks, plane)
    parts = exchange(add_parts(exchange(send, PLANE), depth), "z")
    own, wide = correct(me, first, parts, state)
    update = permute(wide, perm)
    new = write(own, swap(own), mine, other, position, velocity, accel, jerk_old)
    return new + (update,)


def solution(mesh):
    owners = mesh.shape["src"]
    plane = 16
    depth = owners // plane
    fine = Mesh(mesh.devices.reshape(depth, 4, 4, mesh.shape["act"]), ("z", "y", "x", "core"))
    stars = P(None, SRC)
    placed = (stars,) * 4 + (P(SRC),) * 3 + (P("core", None),)
    return jax.shard_map(
        lambda *arrays: local(owners, plane, depth, *arrays),
        mesh=fine,
        in_specs=placed,
        out_specs=(stars,) * 4 + (P(None, "core"),),
        check_vma=False,
    )
```

```python
import jax
import jax.numpy as jnp
from jax import lax
from jax.experimental import pallas as pl
from jax.experimental.pallas import tpu as pltpu
from jax.sharding import Mesh
from jax.sharding import PartitionSpec as P

softening = 0.0025
SLOTS = 64
ROWS = 7
LANES = 128
PLANE = ("y", "x")
SRC = ("z", "y", "x")
F32 = jnp.float32
BF16 = jnp.bfloat16
PREP = 12
PAIRS = ((0, 0), (0, 1), (1, 0), (1, 1), (0, 2), (2, 0))


def params(mebibytes):
    return pltpu.CompilerParams(vmem_limit_bytes=mebibytes << 20)


def cost(microseconds):
    return pl.CostEstimate(flops=0, transcendentals=0, bytes_accessed=microseconds * 3000000)


def vmem():
    return pl.BlockSpec(memory_space=pltpu.VMEM)


def hbm():
    return pl.BlockSpec(memory_space=pltpu.HBM)


def pinned(value):
    return pltpu.with_memory_space_constraint(value, pltpu.HBM)


def smem():
    return pl.BlockSpec(memory_space=pltpu.SMEM)


def three_terms(value):
    high = value.astype(BF16)
    rest = value - high.astype(F32)
    middle = rest.astype(BF16)
    low = (rest - middle.astype(F32)).astype(BF16)
    return high, middle, low


def iota(shape, axis):
    return lax.broadcasted_iota(jnp.int32, shape, axis)


def pick_kernel(me_ref, pos_ref, vel_ref, acc_ref, jrk_ref, mass_ref, phase_ref, level_ref, active_ref,
                send_ref, source_ref, place_ref):
    count = pos_ref.shape[1]
    rows = active_ref.shape[0]
    position, velocity = pos_ref[...], vel_ref[...]
    accel, jerk = acc_ref[...], jrk_ref[...]
    tau = phase_ref[...] * jnp.exp2(-level_ref[...].astype(F32))
    pred_x = position + tau * (velocity + tau * (accel * 0.5 + tau * (jerk / 6.0)))
    pred_v = velocity + tau * (accel + tau * (jerk * 0.5))
    base_x = pred_x - tau * tau * (0.15 * accel + tau * (jerk * (7.0 / 60.0)))
    base_v = pred_v - tau * (0.5 * accel + tau * (jerk * (5.0 / 12.0)))
    source_ref[...] = jnp.concatenate([pred_x, pred_v, mass_ref[...], tau], axis=0)

    offset = active_ref[...] - me_ref[0] * count
    owned = (offset >= 0) & (offset < count)
    flag = jnp.where(owned, 1.0, 0.0)
    before = jnp.where(iota((LANES, LANES), 0) < iota((LANES, LANES), 1), 1.0, 0.0)
    inside = jnp.dot(flag.astype(BF16), before.astype(BF16), preferred_element_type=F32)
    totals = jnp.sum(flag, axis=1, keepdims=True)
    running = jnp.zeros((1, 1), F32)
    place = jnp.zeros((SLOTS, LANES), jnp.int32)
    slot_id = iota((SLOTS, LANES), 0)
    for row in range(rows):
        slot = (inside[row:row + 1] + running).astype(jnp.int32)
        slot = jnp.where(owned[row:row + 1], slot, -1)
        place = place + jnp.where(slot_id == slot, offset[row:row + 1] + 1, 0)
        running = running + totals[row:row + 1]
    spot = jnp.sum(place.astype(F32), axis=1, keepdims=True).astype(jnp.int32) - 1
    place_ref[...] = jnp.broadcast_to(spot, (SLOTS, LANES))

    table = jnp.concatenate([pred_x, pred_v, tau, tau, base_x, base_v, tau, tau], axis=0)
    onehot = jnp.where(iota((SLOTS, count), 1) == spot, 1.0, 0.0).astype(BF16)
    terms = jnp.concatenate(three_terms(table), axis=0)
    picked = lax.dot_general(terms, onehot, (((1,), (1,)), ((), ())), preferred_element_type=F32)
    picked = picked[0:16] + picked[16:32] + picked[32:48]
    block = jnp.concatenate([picked[0:8], picked[8:16]], axis=1)[0:ROWS]
    blocks = jnp.concatenate([block] * 8, axis=0)
    for piece in range(send_ref.shape[0] // (8 * ROWS)):
        send_ref[piece * 8 * ROWS:(piece + 1) * 8 * ROWS] = blocks


def pick(me, position, velocity, accel, jerk_old, masses, phase, levels, active, owners):
    count = position.shape[1]
    return pl.pallas_call(
        pick_kernel,
        out_shape=(
            jax.ShapeDtypeStruct((owners * ROWS, LANES), F32),
            jax.ShapeDtypeStruct((8, count), F32),
            jax.ShapeDtypeStruct((SLOTS, LANES), jnp.int32),
        ),
        in_specs=[smem()] + [vmem()] * 8,
        out_specs=(vmem(), vmem(), vmem()),
        compiler_params=params(56),
        name="pick",
    )(me, position, velocity, accel, jerk_old, masses, phase, levels, active)


def sort_keys(active, count):
    rows = active.shape[0]
    owner = lax.shift_right_logical(active, count.bit_length() - 1)
    return (owner * (rows * LANES) + iota((rows, LANES), 0) * LANES + iota((rows, LANES), 1)).astype(F32)


def prepare_kernel(source_ref, active_ref, first_ref, factor_ref, moment_ref):
    count = source_ref.shape[1]
    rows = active_ref.shape[0]
    total = rows * LANES
    key = sort_keys(active_ref[...], count)
    columns = jnp.transpose(key)
    limit = (iota((1, LANES), 1) * total).astype(F32)
    first = jnp.zeros((8, LANES), F32)
    for row in range(rows):
        column = jnp.broadcast_to(columns[:, row:row + 1], (LANES, LANES))
        first = first + jnp.sum(jnp.where(column < limit, 1.0, 0.0).reshape(LANES // 8, 8, LANES), axis=0)
    first_ref[...] = jnp.sum(first, axis=0, keepdims=True).astype(jnp.int32)

    source = source_ref[...]
    terms = [term.astype(F32) for term in three_terms(source)]
    product = source[0:1] * source[3:4] + source[1:2] * source[4:5] + source[2:3] * source[5:6]
    product = [term.astype(F32) for term in three_terms(product)]
    one = jnp.ones((3, count), F32)
    last = jnp.concatenate(product + [one, jnp.zeros((2, count), F32)], axis=0)
    stack = jnp.concatenate([terms[a] for a, unused in PAIRS] + [last], axis=0)
    mass = source[6:7]
    moments = jnp.concatenate([mass * source[0:6], mass, jnp.zeros((1, count), F32)], axis=0)
    moments = [term.astype(F32) for term in three_terms(moments)]
    moment_ref[...] = jnp.concatenate(moments + [jnp.zeros((8, count), F32)], axis=0).astype(BF16)
    for piece in range(count // LANES):
        here = slice(piece * LANES, (piece + 1) * LANES)
        across = jnp.transpose(stack[:, here])
        factor_ref[here, :] = jnp.concatenate([across, jnp.zeros((LANES, LANES - 56), F32)], axis=1).astype(BF16)


def prepare(source, active):
    count = source.shape[1]
    return pl.pallas_call(
        prepare_kernel,
        out_shape=(
            jax.ShapeDtypeStruct((1, LANES), jnp.int32),
            jax.ShapeDtypeStruct((count, LANES), BF16),
            jax.ShapeDtypeStruct((32, count), BF16),
        ),
        in_specs=[vmem()] * 2,
        out_specs=(vmem(),) * 3,
        compiler_params=params(PREP),
        cost_estimate=cost(5),
        name="prepare",
    )(source, active)


def place(first_ref, states_ref, compact, half, owner):
    start = first_ref[0, owner]
    block = lax.shift_right_logical(start, 7)
    shift = lax.bitwise_and(start, LANES - 1)
    low = owner * ROWS
    if low + 8 <= states_ref.shape[0]:
        value = states_ref[low:low + 8]
    else:
        value = jnp.concatenate([states_ref[low:low + ROWS], jnp.zeros((8 - ROWS, LANES), F32)], axis=0)
    turned = pltpu.roll(value, lax.bitwise_and(shift + half * SLOTS, LANES - 1), 1)
    pltpu.store(compact.at[block], turned, mask=iota((8, LANES), 1) >= shift)
    compact[block + 1] = turned


def tables_kernel(count, active_ref, perm_ref):
    rows = active_ref.shape[0]
    total = rows * LANES
    key = sort_keys(active_ref[...], count)
    columns = jnp.transpose(key)
    ranks = [jnp.zeros((8, LANES), F32) for _ in range(rows)]
    for row in range(rows):
        column = jnp.broadcast_to(columns[:, row:row + 1], (LANES, LANES))
        for to in range(rows):
            less = jnp.where(column < key[to:to + 1], 1.0, 0.0)
            ranks[to] = ranks[to] + jnp.sum(less.reshape(LANES // 8, 8, LANES), axis=0)
    spots = iota((total, LANES), 0)
    for to in range(rows):
        rank = jnp.sum(ranks[to], axis=0, keepdims=True).astype(jnp.int32)
        perm_ref[:, to * LANES:(to + 1) * LANES] = jnp.where(spots == rank, 1.0, 0.0).astype(BF16)


def tables(active, count):
    total = active.shape[0] * LANES
    return pl.pallas_call(
        lambda *refs: tables_kernel(count, *refs),
        out_shape=jax.ShapeDtypeStruct((total, total), BF16),
        in_specs=[vmem()],
        out_specs=vmem(),
        compiler_params=params(8),
        cost_estimate=cost(4),
        name="tables",
    )(active)


def force_kernel(first_hbm, states_ref, factor_ref, moment_ref, send_ref, state_ref,
                 compact, later, first_ref, spread_ref, arrived):
    owners = states_ref.shape[0] // ROWS
    count = factor_ref.shape[0]
    blocks = send_ref.shape[1] // 6
    copy = pltpu.make_async_copy(first_hbm, first_ref, arrived)
    copy.start()
    row, column = iota((LANES, 3 * LANES), 0), iota((LANES, 3 * LANES), 1)
    coordinate = lax.shift_right_logical(column, 7)
    gather = (row == coordinate) | (row == coordinate + 16) | (row == coordinate + 40)
    gather = jnp.where(gather, 1.0, 0.0).astype(BF16)

    def spread(low, size):
        here = pl.ds(low, size)
        wide = jnp.dot(factor_ref[here, :], gather, preferred_element_type=F32)
        for d in range(3):
            spread_ref[d, here, :] = wide[:, d * LANES:(d + 1) * LANES]

    size = count // 8
    spread(0, 4 * size)
    copy.wait()

    spread(4 * size, 4 * size)
    for owner in range(owners):
        place(first_ref, states_ref, compact, 0, owner)
    wide, deep = 2, min(1024, count)
    width = wide * LANES

    def part(block):
        tiles = [compact[block + b] for b in range(wide)]
        star = jnp.concatenate(tiles, axis=1)
        x, v = star[0:3], star[3:6]
        swapped = jnp.concatenate([-v, -x, jnp.zeros((2, width), F32)], axis=0)
        terms = [term.astype(F32) for term in three_terms(swapped)]
        product = [term.astype(F32) for term in three_terms(x[0:1] * v[0:1] + x[1:2] * v[1:2] + x[2:3] * v[2:3])]
        last = jnp.concatenate([jnp.ones((3, width), F32)] + product + [jnp.zeros((2, width), F32)], axis=0)
        cross = jnp.concatenate(
            [terms[b] for unused, b in PAIRS] + [last, jnp.zeros((LANES - 56, width), F32)], axis=0
        ).astype(BF16)
        weighted = jnp.zeros((32, width), F32)
        radial = jnp.zeros((32, width), F32)
        for low in range(0, count, deep):
            here = slice(low, low + deep)
            rel = [jnp.concatenate([spread_ref[d, here, :]] * wide, axis=1) - x[d:d + 1] for d in range(3)]
            dist = rel[0] * rel[0] + rel[1] * rel[1] + (rel[2] * rel[2] + softening)
            inv = lax.rsqrt(dist)
            inv2 = inv * inv
            weight = inv * inv2
            dot = jnp.dot(factor_ref[here, :], cross, preferred_element_type=F32)
            turn = weight * inv2 * dot
            moment = moment_ref[:, here]
            weight_high, turn_high = weight.astype(BF16), turn.astype(BF16)
            weight_low = (weight - weight_high.astype(F32)).astype(BF16)
            turn_low = (turn - turn_high.astype(F32)).astype(BF16)
            weighted = weighted + jnp.dot(moment, weight_high, preferred_element_type=F32)
            weighted = weighted + jnp.dot(moment, weight_low, preferred_element_type=F32)
            radial = radial + jnp.dot(moment, turn_high, preferred_element_type=F32)
            radial = radial + jnp.dot(moment, turn_low, preferred_element_type=F32)
        weighted = weighted[0:8] + weighted[8:16] + weighted[16:24]
        radial = radial[0:8] + radial[8:16] + radial[16:24]
        acc = weighted[0:3] - x * weighted[6:7]
        jrk = weighted[3:6] - v * weighted[6:7] - 3.0 * (radial[0:3] - x * radial[6:7])
        for b in range(wide):
            for d in range(3):
                send_ref[0, pl.ds(d * blocks + block + b, 1), :] = acc[d:d + 1, b * LANES:(b + 1) * LANES]
                send_ref[0, pl.ds((3 + d) * blocks + block + b, 1), :] = jrk[d:d + 1, b * LANES:(b + 1) * LANES]

    for step, block in enumerate(range(0, blocks, wide)):
        part(block)
        share = owners * wide // blocks
        for owner in range(step * share, (step + 1) * share):
            place(first_ref, states_ref, later, 1, owner)
    for field in range(8):
        state_ref[field] = later[0:blocks, field, :]
    for peer in range(1, send_ref.shape[0]):
        send_ref[peer] = send_ref[0]


def forces(first, states, factor, moment, blocks, peers):
    return pl.pallas_call(
        force_kernel,
        out_shape=(
            jax.ShapeDtypeStruct((peers, 6 * blocks, LANES), F32),
            jax.ShapeDtypeStruct((8, blocks, LANES), F32),
        ),
        in_specs=[hbm(), vmem(), vmem(), vmem()],
        out_specs=(vmem(), vmem()),
        scratch_shapes=[
            pltpu.VMEM((blocks + 2, 8, LANES), F32),
            pltpu.VMEM((blocks + 2, 8, LANES), F32),
            pltpu.SMEM(first.shape, first.dtype),
            pltpu.VMEM((3, factor.shape[0], LANES), F32),
            pltpu.SemaphoreType.DMA,
        ],
        compiler_params=params(12),
        cost_estimate=cost(9),
        name="forces",
    )(pinned(first), states, factor, moment)


def add_kernel(parts_ref, send_ref):
    total = jnp.sum(parts_ref[...], axis=0)
    send_ref[...] = jnp.broadcast_to(total[None], send_ref.shape)


def add_parts(parts, peers):
    return pl.pallas_call(
        add_kernel,
        out_shape=jax.ShapeDtypeStruct((peers,) + parts.shape[1:], F32),
        in_specs=[vmem()],
        out_specs=vmem(),
        compiler_params=params(4),
        name="add_parts",
    )(parts)


def correct_kernel(me_ref, first_ref, parts_ref, state_ref, own_ref, wide_ref):
    blocks = state_ref.shape[1]
    total = jnp.sum(parts_ref[...], axis=0)
    tau = state_ref[6]
    t2 = tau * tau
    for d in range(3):
        acc = total[d * blocks:(d + 1) * blocks]
        jrk = total[(3 + d) * blocks:(4 + d) * blocks]
        wide_ref[d, 0:blocks] = state_ref[d] + t2 * (0.15 * acc - tau * (jrk / 30.0))
        wide_ref[3 + d, 0:blocks] = state_ref[3 + d] + tau * (0.5 * acc - tau * (jrk / 12.0))
        wide_ref[6 + d, 0:blocks] = acc
        wide_ref[9 + d, 0:blocks] = jrk
    for f in range(12, 16):
        wide_ref[f, 0:blocks] = jnp.ones_like(tau)
    wide_ref[:, blocks:] = jnp.zeros((16, wide_ref.shape[1] - blocks, LANES), F32)
    start = first_ref[0, me_ref[0]]
    block = lax.shift_right_logical(start, 7)
    shift = lax.bitwise_and(start, LANES - 1)
    back = lax.bitwise_and(LANES - shift, LANES - 1)
    lane = iota((16, LANES), 1)
    low = pltpu.roll(wide_ref[:, block, :], back, 1)
    high = pltpu.roll(wide_ref[:, block + 1, :], back, 1)
    own_ref[...] = jnp.where(lane < LANES - shift, low, high)


def correct(me, first, parts, state):
    blocks = state.shape[1]
    return pl.pallas_call(
        correct_kernel,
        out_shape=(
            jax.ShapeDtypeStruct((16, LANES), F32),
            jax.ShapeDtypeStruct((16, blocks + 2, LANES), F32),
        ),
        in_specs=[smem(), smem(), vmem(), vmem()],
        out_specs=(vmem(), vmem()),
        compiler_params=params(4),
        name="correct",
    )(me, first, parts, state)


def permute_kernel(wide_ref, perm_ref, update_ref):
    blocks = perm_ref.shape[0] // LANES
    value = jnp.concatenate([wide_ref[:, block, :] for block in range(blocks)], axis=1)
    terms = jnp.concatenate(three_terms(value), axis=0)
    result = jnp.dot(terms, perm_ref[...], preferred_element_type=F32)
    update_ref[...] = (result[0:16] + result[16:32] + result[32:48])[0:12]


def permute(wide, perm):
    return pl.pallas_call(
        permute_kernel,
        out_shape=jax.ShapeDtypeStruct((12, perm.shape[1]), F32),
        in_specs=[vmem(), vmem()],
        out_specs=vmem(),
        compiler_params=params(8),
        cost_estimate=cost(2),
        name="permute",
    )(wide, perm)


def write_kernel(mine_ref, other_ref, here_ref, there_ref, pos_ref, vel_ref, acc_ref, jrk_ref,
                 new_pos_ref, new_vel_ref, new_acc_ref, new_jrk_ref):
    count = pos_ref.shape[1]
    both = jnp.concatenate([mine_ref[:, 0:SLOTS], other_ref[:, 0:SLOTS]], axis=1)
    place = jnp.concatenate([here_ref[...], there_ref[...]], axis=0)[:, 0:1]
    onehot = jnp.where(iota((2 * SLOTS, count), 1) == place, 1.0, 0.0).astype(BF16)
    values = jnp.dot(jnp.concatenate(three_terms(both), axis=0), onehot, preferred_element_type=F32)
    values = values[0:16] + values[16:32] + values[32:48]
    hit = values[12:13] > 0.5
    new_pos_ref[...] = jnp.where(hit, values[0:3], pos_ref[...])
    new_vel_ref[...] = jnp.where(hit, values[3:6], vel_ref[...])
    new_acc_ref[...] = jnp.where(hit, values[6:9], acc_ref[...])
    new_jrk_ref[...] = jnp.where(hit, values[9:12], jrk_ref[...])


def write(mine, other, here, there, position, velocity, accel, jerk_old):
    shape = jax.ShapeDtypeStruct(position.shape, F32)
    return pl.pallas_call(
        write_kernel,
        out_shape=(shape,) * 4,
        in_specs=[vmem()] * 8,
        out_specs=(vmem(),) * 4,
        compiler_params=params(4),
        name="write",
    )(mine, other, here, there, position, velocity, accel, jerk_old)


def swap(value):
    return lax.ppermute(value, "core", [(0, 1), (1, 0)])


def exchange(value, axes):
    return lax.all_to_all(value, axes, 0, 0, tiled=True)


def local(owners, plane, depth, position, velocity, accel, jerk_old, masses, phase, levels, active):
    count = position.shape[1]
    blocks = active.shape[0]
    me = lax.axis_index(SRC).reshape(1).astype(jnp.int32)
    send, source, mine = pick(
        me, position, velocity, accel, jerk_old, masses.reshape(1, count), phase.reshape(1, count),
        levels.reshape(1, count), active, owners,
    )
    states = exchange(send.reshape(owners, ROWS, 1, LANES), SRC).reshape(send.shape)
    other = swap(mine)
    first, factor, moment = prepare(source, active)
    perm = tables(active, count)
    states, other, perm = lax.optimization_barrier((states, other, perm))
    send, state = forces(first, states, factor, moment, blocks, plane)
    parts = exchange(add_parts(exchange(send, PLANE), depth), "z")
    own, wide = correct(me, first, parts, state)
    update = permute(wide, perm)
    new = write(own, swap(own), mine, other, position, velocity, accel, jerk_old)
    return new + (update,)


def solution(mesh):
    owners = mesh.shape["src"]
    plane = 16
    depth = owners // plane
    fine = Mesh(mesh.devices.reshape(depth, 4, 4, mesh.shape["act"]), ("z", "y", "x", "core"))
    stars = P(None, SRC)
    placed = (stars,) * 4 + (P(SRC),) * 3 + (P("core", None),)
    return jax.shard_map(
        lambda *arrays: local(owners, plane, depth, *arrays),
        mesh=fine,
        in_specs=placed,
        out_specs=(stars,) * 4 + (P(None, "core"),),
        check_vma=False,
    )
```

```python
import jax
import jax.numpy as jnp
from jax import lax
from jax.experimental import pallas as pl
from jax.experimental.pallas import tpu as pltpu
from jax.sharding import Mesh
from jax.sharding import PartitionSpec as P

softening = 0.0025
SLOTS = 64
ROWS = 7
LANES = 128
PLANE = ("y", "x")
PLANE_SIZE = 16
SRC = ("z", "y", "x")
F32 = jnp.float32
BF16 = jnp.bfloat16
PREP = 12
PAIRS = ((0, 0), (0, 1), (1, 0), (1, 1), (0, 2), (2, 0))


def params(mebibytes):
    return pltpu.CompilerParams(vmem_limit_bytes=mebibytes << 20)


def cost(microseconds):
    return pl.CostEstimate(flops=0, transcendentals=0, bytes_accessed=microseconds * 3000000)


def vmem():
    return pl.BlockSpec(memory_space=pltpu.VMEM)


def hbm():
    return pl.BlockSpec(memory_space=pltpu.HBM)


def pinned(value):
    return pltpu.with_memory_space_constraint(value, pltpu.HBM)


def smem():
    return pl.BlockSpec(memory_space=pltpu.SMEM)


def three_terms(value):
    high = value.astype(BF16)
    rest = value - high.astype(F32)
    middle = rest.astype(BF16)
    low = (rest - middle.astype(F32)).astype(BF16)
    return high, middle, low


def iota(shape, axis):
    return lax.broadcasted_iota(jnp.int32, shape, axis)


def pick_kernel(me_ref, active_hbm, *refs):
    inputs, send_ref, source_ref, place_ref = refs[0:7], refs[7], refs[8], refs[9]
    active_ref, kept, arrived = refs[10], refs[11:18], refs[18]
    copies = [pltpu.make_async_copy(active_hbm, active_ref, arrived.at[7])]
    copies += [pltpu.make_async_copy(here, there, arrived.at[i]) for i, (here, there) in enumerate(zip(inputs, kept))]
    for copy in copies:
        copy.start()
    count = kept[0].shape[1]
    rows = active_ref.shape[0]
    copies[0].wait()
    offset = active_ref[...] - me_ref[0] * count
    owned = (offset >= 0) & (offset < count)
    flag = jnp.where(owned, 1.0, 0.0)
    before = jnp.where(iota((LANES, LANES), 0) < iota((LANES, LANES), 1), 1.0, 0.0)
    inside = jnp.dot(flag.astype(BF16), before.astype(BF16), preferred_element_type=F32)
    totals = jnp.sum(flag, axis=1, keepdims=True)
    running = jnp.zeros((1, 1), F32)
    place = jnp.zeros((SLOTS, LANES), jnp.int32)
    slot_id = iota((SLOTS, LANES), 0)
    for row in range(rows):
        slot = (inside[row:row + 1] + running).astype(jnp.int32)
        slot = jnp.where(owned[row:row + 1], slot, -1)
        place = place + jnp.where(slot_id == slot, offset[row:row + 1] + 1, 0)
        running = running + totals[row:row + 1]
    spot = jnp.sum(place.astype(F32), axis=1, keepdims=True).astype(jnp.int32) - 1
    place_ref[...] = jnp.broadcast_to(spot, (SLOTS, LANES))
    onehot = jnp.where(iota((SLOTS, count), 1) == spot, 1.0, 0.0).astype(BF16)

    for copy in copies[1:]:
        copy.wait()
    position, velocity, accel, jerk, mass, phase, level = [ref[...] for ref in kept]
    tau = phase * jnp.exp2(-level.astype(F32))
    pred_x = position + tau * (velocity + tau * (accel * 0.5 + tau * (jerk / 6.0)))
    pred_v = velocity + tau * (accel + tau * (jerk * 0.5))
    base_x = pred_x - tau * tau * (0.15 * accel + tau * (jerk * (7.0 / 60.0)))
    base_v = pred_v - tau * (0.5 * accel + tau * (jerk * (5.0 / 12.0)))
    source_ref[...] = jnp.concatenate([pred_x, pred_v, mass, tau], axis=0)
    table = jnp.concatenate([pred_x, pred_v, tau, tau, base_x, base_v, tau, tau], axis=0)
    terms = jnp.concatenate(three_terms(table), axis=0)
    picked = lax.dot_general(terms, onehot, (((1,), (1,)), ((), ())), preferred_element_type=F32)
    picked = picked[0:16] + picked[16:32] + picked[32:48]
    block = jnp.concatenate([picked[0:8], picked[8:16]], axis=1)[0:ROWS]
    blocks = jnp.concatenate([block] * (send_ref.shape[0] // ROWS), axis=0)
    send_ref[...] = blocks


def pick(me, position, velocity, accel, jerk_old, masses, phase, levels, active, peers):
    count = position.shape[1]
    inputs = (position, velocity, accel, jerk_old, masses, phase, levels)
    return pl.pallas_call(
        pick_kernel,
        out_shape=(
            jax.ShapeDtypeStruct((peers * ROWS, LANES), F32),
            jax.ShapeDtypeStruct((8, count), F32),
            jax.ShapeDtypeStruct((SLOTS, LANES), jnp.int32),
        ),
        in_specs=[smem()] + [hbm()] * 8,
        out_specs=(vmem(), vmem(), vmem()),
        scratch_shapes=[pltpu.VMEM(value.shape, value.dtype) for value in (active,) + inputs]
        + [pltpu.SemaphoreType.DMA((8,))],
        compiler_params=params(8),
        name="pick",
    )(me, pinned(active), *[pinned(value) for value in inputs])


def sort_keys(active, count):
    rows = active.shape[0]
    owner = lax.shift_right_logical(active, count.bit_length() - 1)
    return (owner * (rows * LANES) + iota((rows, LANES), 0) * LANES + iota((rows, LANES), 1)).astype(F32)


def prepare_kernel(source_ref, active_ref, first_hbm, factor_ref, moment_ref, perm_ref, first_ref, sent):
    count = source_ref.shape[1]
    rows = active_ref.shape[0]
    total = rows * LANES
    key = sort_keys(active_ref[...], count)
    columns = jnp.transpose(key)
    limit = (iota((1, LANES), 1) * total).astype(F32)
    first = jnp.zeros((8, LANES), F32)
    ranks = [jnp.zeros((8, LANES), F32) for _ in range(rows)]
    for row in range(rows):
        column = jnp.broadcast_to(columns[:, row:row + 1], (LANES, LANES))
        first = first + jnp.sum(jnp.where(column < limit, 1.0, 0.0).reshape(LANES // 8, 8, LANES), axis=0)
        for to in range(rows):
            less = jnp.where(column < key[to:to + 1], 1.0, 0.0)
            ranks[to] = ranks[to] + jnp.sum(less.reshape(LANES // 8, 8, LANES), axis=0)
    first_ref[...] = jnp.sum(first, axis=0, keepdims=True).astype(jnp.int32)
    copy = pltpu.make_async_copy(first_ref, first_hbm, sent)
    copy.start()
    spots = iota((total, LANES), 0)
    for to in range(rows):
        rank = jnp.sum(ranks[to], axis=0, keepdims=True).astype(jnp.int32)
        perm_ref[:, to * LANES:(to + 1) * LANES] = jnp.where(spots == rank, 1.0, 0.0).astype(BF16)

    source = source_ref[...]
    terms = [term.astype(F32) for term in three_terms(source)]
    product = source[0:1] * source[3:4] + source[1:2] * source[4:5] + source[2:3] * source[5:6]
    product = [term.astype(F32) for term in three_terms(product)]
    one = jnp.ones((3, count), F32)
    last = jnp.concatenate(product + [one, jnp.zeros((2, count), F32)], axis=0)
    stack = jnp.concatenate([terms[a] for a, unused in PAIRS] + [last], axis=0)
    mass = source[6:7]
    moments = jnp.concatenate([mass * source[0:6], mass, jnp.zeros((1, count), F32)], axis=0)
    moments = [term.astype(F32) for term in three_terms(moments)]
    moment_ref[...] = jnp.concatenate(moments + [jnp.zeros((8, count), F32)], axis=0).astype(BF16)
    for piece in range(count // LANES):
        here = slice(piece * LANES, (piece + 1) * LANES)
        across = jnp.transpose(stack[:, here])
        factor_ref[here, :] = jnp.concatenate([across, jnp.zeros((LANES, LANES - 56), F32)], axis=1).astype(BF16)
    copy.wait()


def prepare(source, active):
    count = source.shape[1]
    total = active.shape[0] * LANES
    return pl.pallas_call(
        prepare_kernel,
        out_shape=(
            jax.ShapeDtypeStruct((1, LANES), jnp.int32),
            jax.ShapeDtypeStruct((count, LANES), BF16),
            jax.ShapeDtypeStruct((32, count), BF16),
            jax.ShapeDtypeStruct((total, total), BF16),
        ),
        in_specs=[vmem()] * 2,
        out_specs=(hbm(),) + (vmem(),) * 3,
        scratch_shapes=[pltpu.VMEM((1, LANES), jnp.int32), pltpu.SemaphoreType.DMA],
        compiler_params=params(12),
        cost_estimate=cost(5),
        name="prepare",
    )(source, active)


def place(first_ref, states_ref, compact, half, owner):
    start = first_ref[0, owner]
    block = lax.shift_right_logical(start, 7)
    shift = lax.bitwise_and(start, LANES - 1)
    depth = states_ref.shape[0] // ROWS // PLANE_SIZE
    low = (owner % PLANE_SIZE * depth + owner // PLANE_SIZE) * ROWS
    if low + 8 <= states_ref.shape[0]:
        value = states_ref[low:low + 8]
    else:
        value = jnp.concatenate([states_ref[low:low + ROWS], jnp.zeros((8 - ROWS, LANES), F32)], axis=0)
    turned = pltpu.roll(value, lax.bitwise_and(shift + half * SLOTS, LANES - 1), 1)
    pltpu.store(compact.at[block], turned, mask=iota((8, LANES), 1) >= shift)
    compact[block + 1] = turned


def force_kernel(first_hbm, states_ref, factor_ref, moment_ref, send_ref, state_ref,
                 compact, later, first_ref, spread_ref, arrived):
    owners = states_ref.shape[0] // ROWS
    count = factor_ref.shape[0]
    blocks = send_ref.shape[1] // 6
    copy = pltpu.make_async_copy(first_hbm, first_ref, arrived)
    copy.start()
    row, column = iota((LANES, 3 * LANES), 0), iota((LANES, 3 * LANES), 1)
    coordinate = lax.shift_right_logical(column, 7)
    gather = (row == coordinate) | (row == coordinate + 16) | (row == coordinate + 40)
    gather = jnp.where(gather, 1.0, 0.0).astype(BF16)

    def spread(low, size):
        here = pl.ds(low, size)
        wide = jnp.dot(factor_ref[here, :], gather, preferred_element_type=F32)
        for d in range(3):
            spread_ref[d, here, :] = wide[:, d * LANES:(d + 1) * LANES]

    size = count // 8
    spread(0, 4 * size)
    copy.wait()

    spread(4 * size, 4 * size)
    for owner in range(owners):
        place(first_ref, states_ref, compact, 0, owner)
    wide, deep = 2, min(1024, count)
    width = wide * LANES

    def part(block):
        tiles = [compact[block + b] for b in range(wide)]
        star = jnp.concatenate(tiles, axis=1)
        x, v = star[0:3], star[3:6]
        swapped = jnp.concatenate([-v, -x, jnp.zeros((2, width), F32)], axis=0)
        terms = [term.astype(F32) for term in three_terms(swapped)]
        product = [term.astype(F32) for term in three_terms(x[0:1] * v[0:1] + x[1:2] * v[1:2] + x[2:3] * v[2:3])]
        last = jnp.concatenate([jnp.ones((3, width), F32)] + product + [jnp.zeros((2, width), F32)], axis=0)
        cross = jnp.concatenate(
            [terms[b] for unused, b in PAIRS] + [last, jnp.zeros((LANES - 56, width), F32)], axis=0
        ).astype(BF16)
        weighted = jnp.zeros((32, width), F32)
        radial = jnp.zeros((32, width), F32)
        for low in range(0, count, deep):
            here = slice(low, low + deep)
            rel = [jnp.concatenate([spread_ref[d, here, :]] * wide, axis=1) - x[d:d + 1] for d in range(3)]
            dist = rel[0] * rel[0] + rel[1] * rel[1] + (rel[2] * rel[2] + softening)
            inv = lax.rsqrt(dist)
            inv2 = inv * inv
            weight = inv * inv2
            dot = jnp.dot(factor_ref[here, :], cross, preferred_element_type=F32)
            turn = weight * inv2 * dot
            moment = moment_ref[:, here]
            weight_high, turn_high = weight.astype(BF16), turn.astype(BF16)
            weight_low = (weight - weight_high.astype(F32)).astype(BF16)
            turn_low = (turn - turn_high.astype(F32)).astype(BF16)
            weighted = weighted + jnp.dot(moment, weight_high, preferred_element_type=F32)
            weighted = weighted + jnp.dot(moment, weight_low, preferred_element_type=F32)
            radial = radial + jnp.dot(moment, turn_high, preferred_element_type=F32)
            radial = radial + jnp.dot(moment, turn_low, preferred_element_type=F32)
        weighted = weighted[0:8] + weighted[8:16] + weighted[16:24]
        radial = radial[0:8] + radial[8:16] + radial[16:24]
        acc = weighted[0:3] - x * weighted[6:7]
        jrk = weighted[3:6] - v * weighted[6:7] - 3.0 * (radial[0:3] - x * radial[6:7])
        for b in range(wide):
            for d in range(3):
                send_ref[0, pl.ds(d * blocks + block + b, 1), :] = acc[d:d + 1, b * LANES:(b + 1) * LANES]
                send_ref[0, pl.ds((3 + d) * blocks + block + b, 1), :] = jrk[d:d + 1, b * LANES:(b + 1) * LANES]

    for step, block in enumerate(range(0, blocks, wide)):
        part(block)
        share = owners * wide // blocks
        for owner in range(step * share, (step + 1) * share):
            place(first_ref, states_ref, later, 1, owner)
    for field in range(8):
        state_ref[field] = later[0:blocks, field, :]
    for peer in range(1, send_ref.shape[0]):
        send_ref[peer] = send_ref[0]


def forces(first, states, factor, moment, blocks, peers):
    return pl.pallas_call(
        force_kernel,
        out_shape=(
            jax.ShapeDtypeStruct((peers, 6 * blocks, LANES), F32),
            jax.ShapeDtypeStruct((8, blocks, LANES), F32),
        ),
        in_specs=[hbm(), vmem(), vmem(), vmem()],
        out_specs=(vmem(), vmem()),
        scratch_shapes=[
            pltpu.VMEM((blocks + 2, 8, LANES), F32),
            pltpu.VMEM((blocks + 2, 8, LANES), F32),
            pltpu.SMEM(first.shape, first.dtype),
            pltpu.VMEM((3, factor.shape[0], LANES), F32),
            pltpu.SemaphoreType.DMA,
        ],
        compiler_params=params(12),
        cost_estimate=cost(9),
        name="forces",
    )(pinned(first), states, factor, moment)


def repeat_kernel(value_ref, send_ref):
    send_ref[...] = jnp.broadcast_to(value_ref[...][None], send_ref.shape)


def repeat(value, peers):
    return pl.pallas_call(
        repeat_kernel,
        out_shape=jax.ShapeDtypeStruct((peers,) + value.shape, F32),
        in_specs=[vmem()],
        out_specs=vmem(),
        compiler_params=params(4),
        name="repeat",
    )(value)


def add_kernel(parts_ref, send_ref):
    total = jnp.sum(parts_ref[...], axis=0)
    send_ref[...] = jnp.broadcast_to(total[None], send_ref.shape)


def add_parts(parts, peers):
    return pl.pallas_call(
        add_kernel,
        out_shape=jax.ShapeDtypeStruct((peers,) + parts.shape[1:], F32),
        in_specs=[vmem()],
        out_specs=vmem(),
        compiler_params=params(4),
        name="add_parts",
    )(parts)


def correct_kernel(me_ref, first_ref, parts_ref, state_ref, own_ref, wide_ref):
    blocks = state_ref.shape[1]
    total = jnp.sum(parts_ref[...], axis=0)
    tau = state_ref[6]
    t2 = tau * tau
    for d in range(3):
        acc = total[d * blocks:(d + 1) * blocks]
        jrk = total[(3 + d) * blocks:(4 + d) * blocks]
        wide_ref[d, 0:blocks] = state_ref[d] + t2 * (0.15 * acc - tau * (jrk / 30.0))
        wide_ref[3 + d, 0:blocks] = state_ref[3 + d] + tau * (0.5 * acc - tau * (jrk / 12.0))
        wide_ref[6 + d, 0:blocks] = acc
        wide_ref[9 + d, 0:blocks] = jrk
    for f in range(12, 16):
        wide_ref[f, 0:blocks] = jnp.ones_like(tau)
    wide_ref[:, blocks:] = jnp.zeros((16, wide_ref.shape[1] - blocks, LANES), F32)
    start = first_ref[0, me_ref[0]]
    block = lax.shift_right_logical(start, 7)
    shift = lax.bitwise_and(start, LANES - 1)
    back = lax.bitwise_and(LANES - shift, LANES - 1)
    lane = iota((16, LANES), 1)
    low = pltpu.roll(wide_ref[:, block, :], back, 1)
    high = pltpu.roll(wide_ref[:, block + 1, :], back, 1)
    own_ref[...] = jnp.where(lane < LANES - shift, low, high)


def correct(me, first, parts, state):
    blocks = state.shape[1]
    return pl.pallas_call(
        correct_kernel,
        out_shape=(
            jax.ShapeDtypeStruct((16, LANES), F32),
            jax.ShapeDtypeStruct((16, blocks + 2, LANES), F32),
        ),
        in_specs=[smem(), smem(), vmem(), vmem()],
        out_specs=(vmem(), vmem()),
        compiler_params=params(4),
        name="correct",
    )(me, first, parts, state)


def permute_kernel(wide_ref, perm_ref, update_ref):
    blocks = perm_ref.shape[0] // LANES
    value = jnp.concatenate([wide_ref[:, block, :] for block in range(blocks)], axis=1)
    terms = jnp.concatenate(three_terms(value), axis=0)
    result = jnp.dot(terms, perm_ref[...], preferred_element_type=F32)
    update_ref[...] = (result[0:16] + result[16:32] + result[32:48])[0:12]


def permute(wide, perm):
    return pl.pallas_call(
        permute_kernel,
        out_shape=jax.ShapeDtypeStruct((12, perm.shape[1]), F32),
        in_specs=[vmem(), vmem()],
        out_specs=vmem(),
        compiler_params=params(8),
        cost_estimate=cost(2),
        name="permute",
    )(wide, perm)


def write_kernel(mine_ref, other_ref, here_ref, there_ref, pos_ref, vel_ref, acc_ref, jrk_ref,
                 new_pos_ref, new_vel_ref, new_acc_ref, new_jrk_ref):
    count = pos_ref.shape[1]
    both = jnp.concatenate([mine_ref[:, 0:SLOTS], other_ref[:, 0:SLOTS]], axis=1)
    place = jnp.concatenate([here_ref[...], there_ref[...]], axis=0)[:, 0:1]
    onehot = jnp.where(iota((2 * SLOTS, count), 1) == place, 1.0, 0.0).astype(BF16)
    values = jnp.dot(jnp.concatenate(three_terms(both), axis=0), onehot, preferred_element_type=F32)
    values = values[0:16] + values[16:32] + values[32:48]
    hit = values[12:13] > 0.5
    new_pos_ref[...] = jnp.where(hit, values[0:3], pos_ref[...])
    new_vel_ref[...] = jnp.where(hit, values[3:6], vel_ref[...])
    new_acc_ref[...] = jnp.where(hit, values[6:9], acc_ref[...])
    new_jrk_ref[...] = jnp.where(hit, values[9:12], jrk_ref[...])


def write(mine, other, here, there, position, velocity, accel, jerk_old):
    shape = jax.ShapeDtypeStruct(position.shape, F32)
    return pl.pallas_call(
        write_kernel,
        out_shape=(shape,) * 4,
        in_specs=[vmem()] * 8,
        out_specs=(vmem(),) * 4,
        compiler_params=params(4),
        name="write",
    )(mine, other, here, there, position, velocity, accel, jerk_old)


def swap(value):
    return lax.ppermute(value, "core", [(0, 1), (1, 0)])


def exchange(value, axes):
    return lax.all_to_all(value, axes, 0, 0, tiled=True)


def local(owners, plane, depth, position, velocity, accel, jerk_old, masses, phase, levels, active):
    count = position.shape[1]
    blocks = active.shape[0]
    me = lax.axis_index(SRC).reshape(1).astype(jnp.int32)
    send, source, mine = pick(
        me, position, velocity, accel, jerk_old, masses.reshape(1, count), phase.reshape(1, count),
        levels.reshape(1, count), active, depth,
    )
    column = exchange(send.reshape(depth, ROWS, 1, LANES), "z").reshape(send.shape)
    other = swap(mine)
    first, factor, moment, perm = prepare(source, active)
    column, other, perm, factor = lax.optimization_barrier((column, other, perm, factor))
    states = exchange(repeat(column, plane), PLANE).reshape(owners * ROWS, LANES)
    send, state = forces(first, states, factor, moment, blocks, plane)
    parts = exchange(add_parts(exchange(send, PLANE), depth), "z")
    own, wide = correct(me, first, parts, state)
    update = permute(wide, perm)
    new = write(own, swap(own), mine, other, position, velocity, accel, jerk_old)
    return new + (update,)


def solution(mesh):
    owners = mesh.shape["src"]
    plane = PLANE_SIZE
    depth = owners // plane
    fine = Mesh(mesh.devices.reshape(depth, 4, 4, mesh.shape["act"]), ("z", "y", "x", "core"))
    stars = P(None, SRC)
    placed = (stars,) * 4 + (P(SRC),) * 3 + (P("core", None),)
    return jax.shard_map(
        lambda *arrays: local(owners, plane, depth, *arrays),
        mesh=fine,
        in_specs=placed,
        out_specs=(stars,) * 4 + (P(None, "core"),),
        check_vma=False,
    )
```

```python
import jax
import jax.numpy as jnp
from jax import lax
from jax.experimental import pallas as pl
from jax.experimental.pallas import tpu as pltpu
from jax.sharding import Mesh
from jax.sharding import PartitionSpec as P

softening = 0.0025
SLOTS = 64
ROWS = 7
LANES = 128
PLANE = ("y", "x")
PLANE_SIZE = 16
SRC = ("z", "y", "x")
F32 = jnp.float32
BF16 = jnp.bfloat16
PREP = 12
PAIRS = ((0, 0), (0, 1), (1, 0), (1, 1), (0, 2), (2, 0))


def params(mebibytes):
    return pltpu.CompilerParams(vmem_limit_bytes=mebibytes << 20)


def cost(microseconds):
    return pl.CostEstimate(flops=0, transcendentals=0, bytes_accessed=microseconds * 3000000)


def vmem():
    return pl.BlockSpec(memory_space=pltpu.VMEM)


def hbm():
    return pl.BlockSpec(memory_space=pltpu.HBM)


def pinned(value):
    return pltpu.with_memory_space_constraint(value, pltpu.HBM)


def smem():
    return pl.BlockSpec(memory_space=pltpu.SMEM)


def three_terms(value):
    high = value.astype(BF16)
    rest = value - high.astype(F32)
    middle = rest.astype(BF16)
    low = (rest - middle.astype(F32)).astype(BF16)
    return high, middle, low


def iota(shape, axis):
    return lax.broadcasted_iota(jnp.int32, shape, axis)


def pick_kernel(me_ref, active_hbm, *refs):
    inputs, send_ref, source_ref, place_ref = refs[0:7], refs[7], refs[8], refs[9]
    active_ref, kept, arrived = refs[10], refs[11:18], refs[18]
    copies = [pltpu.make_async_copy(active_hbm, active_ref, arrived.at[7])]
    copies += [pltpu.make_async_copy(here, there, arrived.at[i]) for i, (here, there) in enumerate(zip(inputs, kept))]
    for copy in copies:
        copy.start()
    count = kept[0].shape[1]
    rows = active_ref.shape[0]
    copies[0].wait()
    offset = active_ref[...] - me_ref[0] * count
    owned = (offset >= 0) & (offset < count)
    flag = jnp.where(owned, 1.0, 0.0)
    before = jnp.where(iota((LANES, LANES), 0) < iota((LANES, LANES), 1), 1.0, 0.0)
    inside = jnp.dot(flag.astype(BF16), before.astype(BF16), preferred_element_type=F32)
    totals = jnp.sum(flag, axis=1, keepdims=True)
    running = jnp.zeros((1, 1), F32)
    place = jnp.zeros((SLOTS, LANES), jnp.int32)
    slot_id = iota((SLOTS, LANES), 0)
    for row in range(rows):
        slot = (inside[row:row + 1] + running).astype(jnp.int32)
        slot = jnp.where(owned[row:row + 1], slot, -1)
        place = place + jnp.where(slot_id == slot, offset[row:row + 1] + 1, 0)
        running = running + totals[row:row + 1]
    spot = jnp.sum(place.astype(F32), axis=1, keepdims=True).astype(jnp.int32) - 1
    place_ref[...] = jnp.broadcast_to(spot, (SLOTS, LANES))
    onehot = jnp.where(iota((SLOTS, count), 1) == spot, 1.0, 0.0).astype(BF16)

    for copy in copies[1:]:
        copy.wait()
    position, velocity, accel, jerk, mass, phase, level = [ref[...] for ref in kept]
    tau = phase * jnp.exp2(-level.astype(F32))
    pred_x = position + tau * (velocity + tau * (accel * 0.5 + tau * (jerk / 6.0)))
    pred_v = velocity + tau * (accel + tau * (jerk * 0.5))
    base_x = pred_x - tau * tau * (0.15 * accel + tau * (jerk * (7.0 / 60.0)))
    base_v = pred_v - tau * (0.5 * accel + tau * (jerk * (5.0 / 12.0)))
    source_ref[...] = jnp.concatenate([pred_x, pred_v, mass, tau], axis=0)
    table = jnp.concatenate([pred_x, pred_v, tau, tau, base_x, base_v, tau, tau], axis=0)
    terms = jnp.concatenate(three_terms(table), axis=0)
    picked = lax.dot_general(terms, onehot, (((1,), (1,)), ((), ())), preferred_element_type=F32)
    picked = picked[0:16] + picked[16:32] + picked[32:48]
    block = jnp.concatenate([picked[0:8], picked[8:16]], axis=1)[0:ROWS]
    blocks = jnp.concatenate([block] * (send_ref.shape[0] // ROWS), axis=0)
    send_ref[...] = blocks


def pick(me, position, velocity, accel, jerk_old, masses, phase, levels, active, peers):
    count = position.shape[1]
    inputs = (position, velocity, accel, jerk_old, masses, phase, levels)
    return pl.pallas_call(
        pick_kernel,
        out_shape=(
            jax.ShapeDtypeStruct((peers * ROWS, LANES), F32),
            jax.ShapeDtypeStruct((8, count), F32),
            jax.ShapeDtypeStruct((SLOTS, LANES), jnp.int32),
        ),
        in_specs=[smem()] + [hbm()] * 8,
        out_specs=(vmem(), vmem(), vmem()),
        scratch_shapes=[pltpu.VMEM(value.shape, value.dtype) for value in (active,) + inputs]
        + [pltpu.SemaphoreType.DMA((8,))],
        compiler_params=params(8),
        name="pick",
    )(me, pinned(active), *[pinned(value) for value in inputs])


def sort_keys(active, count):
    rows = active.shape[0]
    owner = lax.shift_right_logical(active, count.bit_length() - 1)
    return (owner * (rows * LANES) + iota((rows, LANES), 0) * LANES + iota((rows, LANES), 1)).astype(F32)


def prepare_kernel(source_ref, active_ref, first_hbm, factor_ref, moment_ref, perm_ref, first_ref, sent):
    count = source_ref.shape[1]
    rows = active_ref.shape[0]
    total = rows * LANES
    key = sort_keys(active_ref[...], count)
    columns = jnp.transpose(key)
    limit = (iota((1, LANES), 1) * total).astype(F32)
    first = jnp.zeros((8, LANES), F32)
    ranks = [jnp.zeros((8, LANES), F32) for _ in range(rows)]
    for row in range(rows):
        column = jnp.broadcast_to(columns[:, row:row + 1], (LANES, LANES))
        first = first + jnp.sum(jnp.where(column < limit, 1.0, 0.0).reshape(LANES // 8, 8, LANES), axis=0)
        for to in range(rows):
            less = jnp.where(column < key[to:to + 1], 1.0, 0.0)
            ranks[to] = ranks[to] + jnp.sum(less.reshape(LANES // 8, 8, LANES), axis=0)
    first_ref[...] = jnp.sum(first, axis=0, keepdims=True).astype(jnp.int32)
    copy = pltpu.make_async_copy(first_ref, first_hbm, sent)
    copy.start()
    spots = iota((total, LANES), 0)
    for to in range(rows):
        rank = jnp.sum(ranks[to], axis=0, keepdims=True).astype(jnp.int32)
        perm_ref[:, to * LANES:(to + 1) * LANES] = jnp.where(spots == rank, 1.0, 0.0).astype(BF16)

    source = source_ref[...]
    terms = [term.astype(F32) for term in three_terms(source)]
    product = source[0:1] * source[3:4] + source[1:2] * source[4:5] + source[2:3] * source[5:6]
    product = [term.astype(F32) for term in three_terms(product)]
    one = jnp.ones((3, count), F32)
    last = jnp.concatenate(product + [one, jnp.zeros((2, count), F32)], axis=0)
    stack = jnp.concatenate([terms[a] for a, unused in PAIRS] + [last], axis=0)
    mass = source[6:7]
    moments = jnp.concatenate([mass * source[0:6], mass, jnp.zeros((1, count), F32)], axis=0)
    moments = [term.astype(F32) for term in three_terms(moments)]
    moment_ref[...] = jnp.concatenate(moments + [jnp.zeros((8, count), F32)], axis=0).astype(BF16)
    for piece in range(count // LANES):
        here = slice(piece * LANES, (piece + 1) * LANES)
        across = jnp.transpose(stack[:, here])
        factor_ref[here, :] = jnp.concatenate([across, jnp.zeros((LANES, LANES - 56), F32)], axis=1).astype(BF16)
    copy.wait()


def prepare(source, active):
    count = source.shape[1]
    total = active.shape[0] * LANES
    return pl.pallas_call(
        prepare_kernel,
        out_shape=(
            jax.ShapeDtypeStruct((1, LANES), jnp.int32),
            jax.ShapeDtypeStruct((count, LANES), BF16),
            jax.ShapeDtypeStruct((32, count), BF16),
            jax.ShapeDtypeStruct((total, total), BF16),
        ),
        in_specs=[vmem()] * 2,
        out_specs=(hbm(),) + (vmem(),) * 3,
        scratch_shapes=[pltpu.VMEM((1, LANES), jnp.int32), pltpu.SemaphoreType.DMA],
        compiler_params=params(12),
        cost_estimate=cost(5),
        name="prepare",
    )(source, active)


def place(first_ref, states_ref, compact, half, owner):
    start = first_ref[0, owner]
    block = lax.shift_right_logical(start, 7)
    shift = lax.bitwise_and(start, LANES - 1)
    depth = states_ref.shape[0] // ROWS // PLANE_SIZE
    low = (owner % PLANE_SIZE * depth + owner // PLANE_SIZE) * ROWS
    if low + 8 <= states_ref.shape[0]:
        value = states_ref[low:low + 8]
    else:
        value = jnp.concatenate([states_ref[low:low + ROWS], jnp.zeros((8 - ROWS, LANES), F32)], axis=0)
    turned = pltpu.roll(value, lax.bitwise_and(shift + half * SLOTS, LANES - 1), 1)
    pltpu.store(compact.at[block], turned, mask=iota((8, LANES), 1) >= shift)
    compact[block + 1] = turned


def force_kernel(first_hbm, states_ref, factor_ref, moment_ref, send_ref, state_ref,
                 compact, later, first_ref, spread_ref, arrived):
    owners = states_ref.shape[0] // ROWS
    count = factor_ref.shape[0]
    blocks = send_ref.shape[1] // 6
    copy = pltpu.make_async_copy(first_hbm, first_ref, arrived)
    copy.start()
    row, column = iota((LANES, 3 * LANES), 0), iota((LANES, 3 * LANES), 1)
    coordinate = lax.shift_right_logical(column, 7)
    gather = (row == coordinate) | (row == coordinate + 16) | (row == coordinate + 40)
    gather = jnp.where(gather, 1.0, 0.0).astype(BF16)

    def spread(low, size):
        here = pl.ds(low, size)
        wide = jnp.dot(factor_ref[here, :], gather, preferred_element_type=F32)
        for d in range(3):
            spread_ref[d, here, :] = wide[:, d * LANES:(d + 1) * LANES]

    size = count // 8
    spread(0, 4 * size)
    copy.wait()

    spread(4 * size, 4 * size)
    for owner in range(owners):
        place(first_ref, states_ref, compact, 0, owner)
    wide, deep = 2, min(1024, count)
    width = wide * LANES

    def part(block):
        tiles = [compact[block + b] for b in range(wide)]
        star = jnp.concatenate(tiles, axis=1)
        x, v = star[0:3], star[3:6]
        swapped = jnp.concatenate([-v, -x, jnp.zeros((2, width), F32)], axis=0)
        terms = [term.astype(F32) for term in three_terms(swapped)]
        product = [term.astype(F32) for term in three_terms(x[0:1] * v[0:1] + x[1:2] * v[1:2] + x[2:3] * v[2:3])]
        last = jnp.concatenate([jnp.ones((3, width), F32)] + product + [jnp.zeros((2, width), F32)], axis=0)
        cross = jnp.concatenate(
            [terms[b] for unused, b in PAIRS] + [last, jnp.zeros((LANES - 56, width), F32)], axis=0
        ).astype(BF16)
        weighted = jnp.zeros((32, width), F32)
        radial = jnp.zeros((32, width), F32)
        for low in range(0, count, deep):
            here = slice(low, low + deep)
            rel = [jnp.concatenate([spread_ref[d, here, :]] * wide, axis=1) - x[d:d + 1] for d in range(3)]
            dist = rel[0] * rel[0] + rel[1] * rel[1] + (rel[2] * rel[2] + softening)
            inv = lax.rsqrt(dist)
            inv2 = inv * inv
            weight = inv * inv2
            dot = jnp.dot(factor_ref[here, :], cross, preferred_element_type=F32)
            turn = weight * inv2 * dot
            moment = moment_ref[:, here]
            weight_high, turn_high = weight.astype(BF16), turn.astype(BF16)
            weight_low = (weight - weight_high.astype(F32)).astype(BF16)
            turn_low = (turn - turn_high.astype(F32)).astype(BF16)
            weighted = weighted + jnp.dot(moment, weight_high, preferred_element_type=F32)
            weighted = weighted + jnp.dot(moment, weight_low, preferred_element_type=F32)
            radial = radial + jnp.dot(moment, turn_high, preferred_element_type=F32)
            radial = radial + jnp.dot(moment, turn_low, preferred_element_type=F32)
        weighted = weighted[0:8] + weighted[8:16] + weighted[16:24]
        radial = radial[0:8] + radial[8:16] + radial[16:24]
        acc = weighted[0:3] - x * weighted[6:7]
        jrk = weighted[3:6] - v * weighted[6:7] - 3.0 * (radial[0:3] - x * radial[6:7])
        for b in range(wide):
            for d in range(3):
                send_ref[0, pl.ds(d * blocks + block + b, 1), :] = acc[d:d + 1, b * LANES:(b + 1) * LANES]
                send_ref[0, pl.ds((3 + d) * blocks + block + b, 1), :] = jrk[d:d + 1, b * LANES:(b + 1) * LANES]

    for step, block in enumerate(range(0, blocks, wide)):
        part(block)
        share = owners * wide // blocks
        for owner in range(step * share, (step + 1) * share):
            place(first_ref, states_ref, later, 1, owner)
    for field in range(8):
        state_ref[field] = later[0:blocks, field, :]
    for peer in range(1, send_ref.shape[0]):
        send_ref[peer] = send_ref[0]


def forces(first, states, factor, moment, blocks, peers):
    return pl.pallas_call(
        force_kernel,
        out_shape=(
            jax.ShapeDtypeStruct((peers, 6 * blocks, LANES), F32),
            jax.ShapeDtypeStruct((8, blocks, LANES), F32),
        ),
        in_specs=[hbm(), vmem(), vmem(), vmem()],
        out_specs=(vmem(), vmem()),
        scratch_shapes=[
            pltpu.VMEM((blocks + 2, 8, LANES), F32),
            pltpu.VMEM((blocks + 2, 8, LANES), F32),
            pltpu.SMEM(first.shape, first.dtype),
            pltpu.VMEM((3, factor.shape[0], LANES), F32),
            pltpu.SemaphoreType.DMA,
        ],
        compiler_params=params(12),
        cost_estimate=cost(9),
        name="forces",
    )(pinned(first), states, factor, moment)


def repeat_kernel(value_ref, send_ref):
    send_ref[...] = jnp.broadcast_to(value_ref[...][None], send_ref.shape)


def repeat(value, peers):
    return pl.pallas_call(
        repeat_kernel,
        out_shape=jax.ShapeDtypeStruct((peers,) + value.shape, F32),
        in_specs=[vmem()],
        out_specs=vmem(),
        compiler_params=params(4),
        name="repeat",
    )(value)


def add_kernel(parts_ref, send_ref):
    total = jnp.sum(parts_ref[...], axis=0)
    send_ref[...] = jnp.broadcast_to(total[None], send_ref.shape)


def add_parts(parts, peers):
    return pl.pallas_call(
        add_kernel,
        out_shape=jax.ShapeDtypeStruct((peers,) + parts.shape[1:], F32),
        in_specs=[vmem()],
        out_specs=vmem(),
        compiler_params=params(4),
        name="add_parts",
    )(parts)


def correct_kernel(me_ref, first_ref, parts_ref, state_ref, own_ref, wide_ref):
    blocks = state_ref.shape[1]
    total = jnp.sum(parts_ref[...], axis=0)
    tau = state_ref[6]
    t2 = tau * tau
    for d in range(3):
        acc = total[d * blocks:(d + 1) * blocks]
        jrk = total[(3 + d) * blocks:(4 + d) * blocks]
        wide_ref[d, 0:blocks] = state_ref[d] + t2 * (0.15 * acc - tau * (jrk / 30.0))
        wide_ref[3 + d, 0:blocks] = state_ref[3 + d] + tau * (0.5 * acc - tau * (jrk / 12.0))
        wide_ref[6 + d, 0:blocks] = acc
        wide_ref[9 + d, 0:blocks] = jrk
    for f in range(12, 16):
        wide_ref[f, 0:blocks] = jnp.ones_like(tau)
    wide_ref[:, blocks:] = jnp.zeros((16, wide_ref.shape[1] - blocks, LANES), F32)
    start = first_ref[0, me_ref[0]]
    block = lax.shift_right_logical(start, 7)
    shift = lax.bitwise_and(start, LANES - 1)
    back = lax.bitwise_and(LANES - shift, LANES - 1)
    lane = iota((16, LANES), 1)
    low = pltpu.roll(wide_ref[:, block, :], back, 1)
    high = pltpu.roll(wide_ref[:, block + 1, :], back, 1)
    own_ref[...] = jnp.where(lane < LANES - shift, low, high)


def correct(me, first, parts, state):
    blocks = state.shape[1]
    return pl.pallas_call(
        correct_kernel,
        out_shape=(
            jax.ShapeDtypeStruct((16, LANES), F32),
            jax.ShapeDtypeStruct((16, blocks + 2, LANES), F32),
        ),
        in_specs=[smem(), smem(), vmem(), vmem()],
        out_specs=(vmem(), vmem()),
        compiler_params=params(4),
        name="correct",
    )(me, first, parts, state)


def permute_kernel(wide_ref, perm_ref, update_ref):
    blocks = perm_ref.shape[0] // LANES
    value = jnp.concatenate([wide_ref[:, block, :] for block in range(blocks)], axis=1)
    terms = jnp.concatenate(three_terms(value), axis=0)
    result = jnp.dot(terms, perm_ref[...], preferred_element_type=F32)
    update_ref[...] = (result[0:16] + result[16:32] + result[32:48])[0:12]


def permute(wide, perm):
    return pl.pallas_call(
        permute_kernel,
        out_shape=jax.ShapeDtypeStruct((12, perm.shape[1]), F32),
        in_specs=[vmem(), vmem()],
        out_specs=vmem(),
        compiler_params=params(8),
        cost_estimate=cost(2),
        name="permute",
    )(wide, perm)


def write_kernel(mine_ref, other_ref, here_ref, there_ref, pos_ref, vel_ref, acc_ref, jrk_ref,
                 new_pos_ref, new_vel_ref, new_acc_ref, new_jrk_ref):
    count = pos_ref.shape[1]
    both = jnp.concatenate([mine_ref[:, 0:SLOTS], other_ref[:, 0:SLOTS]], axis=1)
    place = jnp.concatenate([here_ref[...], there_ref[...]], axis=0)[:, 0:1]
    onehot = jnp.where(iota((2 * SLOTS, count), 1) == place, 1.0, 0.0).astype(BF16)
    values = jnp.dot(jnp.concatenate(three_terms(both), axis=0), onehot, preferred_element_type=F32)
    values = values[0:16] + values[16:32] + values[32:48]
    hit = values[12:13] > 0.5
    new_pos_ref[...] = jnp.where(hit, values[0:3], pos_ref[...])
    new_vel_ref[...] = jnp.where(hit, values[3:6], vel_ref[...])
    new_acc_ref[...] = jnp.where(hit, values[6:9], acc_ref[...])
    new_jrk_ref[...] = jnp.where(hit, values[9:12], jrk_ref[...])


def write(mine, other, here, there, position, velocity, accel, jerk_old):
    shape = jax.ShapeDtypeStruct(position.shape, F32)
    return pl.pallas_call(
        write_kernel,
        out_shape=(shape,) * 4,
        in_specs=[vmem()] * 8,
        out_specs=(vmem(),) * 4,
        compiler_params=params(4),
        name="write",
    )(mine, other, here, there, position, velocity, accel, jerk_old)


def swap(value):
    return lax.ppermute(value, "core", [(0, 1), (1, 0)])


def exchange(value, axes):
    return lax.all_to_all(value, axes, 0, 0, tiled=True)


def local(owners, plane, depth, position, velocity, accel, jerk_old, masses, phase, levels, active):
    count = position.shape[1]
    blocks = active.shape[0]
    me = lax.axis_index(SRC).reshape(1).astype(jnp.int32)
    send, source, mine = pick(
        me, position, velocity, accel, jerk_old, masses.reshape(1, count), phase.reshape(1, count),
        levels.reshape(1, count), active, depth,
    )
    column = exchange(send.reshape(depth, ROWS, 1, LANES), "z").reshape(send.shape)
    column, late, mine = lax.optimization_barrier((column, active, mine))
    states = exchange(repeat(column, plane), PLANE).reshape(owners * ROWS, LANES)
    other = swap(mine)
    first, factor, moment, perm = prepare(source, late)
    states, other, perm = lax.optimization_barrier((states, other, perm))
    send, state = forces(first, states, factor, moment, blocks, plane)
    parts = exchange(add_parts(exchange(send, PLANE), depth), "z")
    own, wide = correct(me, first, parts, state)
    update = permute(wide, perm)
    new = write(own, swap(own), mine, other, position, velocity, accel, jerk_old)
    return new + (update,)


def solution(mesh):
    owners = mesh.shape["src"]
    plane = PLANE_SIZE
    depth = owners // plane
    fine = Mesh(mesh.devices.reshape(depth, 4, 4, mesh.shape["act"]), ("z", "y", "x", "core"))
    stars = P(None, SRC)
    placed = (stars,) * 4 + (P(SRC),) * 3 + (P("core", None),)
    return jax.shard_map(
        lambda *arrays: local(owners, plane, depth, *arrays),
        mesh=fine,
        in_specs=placed,
        out_specs=(stars,) * 4 + (P(None, "core"),),
        check_vma=False,
    )
```

```python
import jax
import jax.numpy as jnp
from jax import lax
from jax.experimental import pallas as pl
from jax.experimental.pallas import tpu as pltpu
from jax.sharding import Mesh
from jax.sharding import PartitionSpec as P

softening = 0.0025
SLOTS = 64
ROWS = 7
LANES = 128
PLANE = ("y", "x")
PLANE_SIZE = 16
SRC = ("z", "y", "x")
F32 = jnp.float32
BF16 = jnp.bfloat16
PREP = 12
PAIRS = ((0, 0), (0, 1), (1, 0), (1, 1), (0, 2), (2, 0))


def params(mebibytes):
    return pltpu.CompilerParams(vmem_limit_bytes=mebibytes << 20)


def cost(microseconds):
    return pl.CostEstimate(flops=0, transcendentals=0, bytes_accessed=microseconds * 3000000)


def vmem():
    return pl.BlockSpec(memory_space=pltpu.VMEM)


def hbm():
    return pl.BlockSpec(memory_space=pltpu.HBM)


def pinned(value):
    return pltpu.with_memory_space_constraint(value, pltpu.HBM)


def smem():
    return pl.BlockSpec(memory_space=pltpu.SMEM)


def three_terms(value):
    high = value.astype(BF16)
    rest = value - high.astype(F32)
    middle = rest.astype(BF16)
    low = (rest - middle.astype(F32)).astype(BF16)
    return high, middle, low


def iota(shape, axis):
    return lax.broadcasted_iota(jnp.int32, shape, axis)


def pick_kernel(me_ref, active_hbm, *refs):
    inputs, send_ref, source_ref, place_ref = refs[0:7], refs[7], refs[8], refs[9]
    active_ref, kept, arrived = refs[10], refs[11:18], refs[18]
    copies = [pltpu.make_async_copy(active_hbm, active_ref, arrived.at[7])]
    copies += [pltpu.make_async_copy(here, there, arrived.at[i]) for i, (here, there) in enumerate(zip(inputs, kept))]
    for copy in copies:
        copy.start()
    count = kept[0].shape[1]
    rows = active_ref.shape[0]
    copies[0].wait()
    offset = active_ref[...] - me_ref[0] * count
    owned = (offset >= 0) & (offset < count)
    flag = jnp.where(owned, 1.0, 0.0)
    before = jnp.where(iota((LANES, LANES), 0) < iota((LANES, LANES), 1), 1.0, 0.0)
    inside = jnp.dot(flag.astype(BF16), before.astype(BF16), preferred_element_type=F32)
    totals = jnp.sum(flag, axis=1, keepdims=True)
    running = jnp.zeros((1, 1), F32)
    place = jnp.zeros((SLOTS, LANES), jnp.int32)
    slot_id = iota((SLOTS, LANES), 0)
    for row in range(rows):
        slot = (inside[row:row + 1] + running).astype(jnp.int32)
        slot = jnp.where(owned[row:row + 1], slot, -1)
        place = place + jnp.where(slot_id == slot, offset[row:row + 1] + 1, 0)
        running = running + totals[row:row + 1]
    spot = jnp.sum(place.astype(F32), axis=1, keepdims=True).astype(jnp.int32) - 1
    place_ref[...] = jnp.broadcast_to(spot, (SLOTS, LANES))
    onehot = jnp.where(iota((SLOTS, count), 1) == spot, 1.0, 0.0).astype(BF16)

    for copy in copies[1:]:
        copy.wait()
    position, velocity, accel, jerk, mass, phase, level = [ref[...] for ref in kept]
    tau = phase * jnp.exp2(-level.astype(F32))
    pred_x = position + tau * (velocity + tau * (accel * 0.5 + tau * (jerk / 6.0)))
    pred_v = velocity + tau * (accel + tau * (jerk * 0.5))
    base_x = pred_x - tau * tau * (0.15 * accel + tau * (jerk * (7.0 / 60.0)))
    base_v = pred_v - tau * (0.5 * accel + tau * (jerk * (5.0 / 12.0)))
    source_ref[...] = jnp.concatenate([pred_x, pred_v, mass, tau], axis=0)
    table = jnp.concatenate([pred_x, pred_v, tau, tau, base_x, base_v, tau, tau], axis=0)
    terms = jnp.concatenate(three_terms(table), axis=0)
    picked = lax.dot_general(terms, onehot, (((1,), (1,)), ((), ())), preferred_element_type=F32)
    picked = picked[0:16] + picked[16:32] + picked[32:48]
    block = jnp.concatenate([picked[0:8], picked[8:16]], axis=1)[0:ROWS]
    blocks = jnp.concatenate([block] * (send_ref.shape[0] // ROWS), axis=0)
    send_ref[...] = blocks


def pick(me, position, velocity, accel, jerk_old, masses, phase, levels, active, peers):
    count = position.shape[1]
    inputs = (position, velocity, accel, jerk_old, masses, phase, levels)
    return pl.pallas_call(
        pick_kernel,
        out_shape=(
            jax.ShapeDtypeStruct((peers * ROWS, LANES), F32),
            jax.ShapeDtypeStruct((8, count), F32),
            jax.ShapeDtypeStruct((SLOTS, LANES), jnp.int32),
        ),
        in_specs=[smem()] + [hbm()] * 8,
        out_specs=(vmem(), vmem(), vmem()),
        scratch_shapes=[pltpu.VMEM(value.shape, value.dtype) for value in (active,) + inputs]
        + [pltpu.SemaphoreType.DMA((8,))],
        compiler_params=params(8),
        name="pick",
    )(me, pinned(active), *[pinned(value) for value in inputs])


def sort_keys(active, count):
    rows = active.shape[0]
    owner = lax.shift_right_logical(active, count.bit_length() - 1)
    return (owner * (rows * LANES) + iota((rows, LANES), 0) * LANES + iota((rows, LANES), 1)).astype(F32)


def prepare_kernel(me_ref, source_ref, active_ref, first_hbm, factor_ref, moment_ref, perm_ref, select_ref,
                   first_ref, sent):
    count = source_ref.shape[1]
    rows = active_ref.shape[0]
    total = rows * LANES
    key = sort_keys(active_ref[...], count)
    columns = jnp.transpose(key)
    limit = (iota((1, LANES), 1) * total).astype(F32)
    first = jnp.zeros((8, LANES), F32)
    ranks = [jnp.zeros((8, LANES), F32) for _ in range(rows)]
    for row in range(rows):
        column = jnp.broadcast_to(columns[:, row:row + 1], (LANES, LANES))
        first = first + jnp.sum(jnp.where(column < limit, 1.0, 0.0).reshape(LANES // 8, 8, LANES), axis=0)
        for to in range(rows):
            less = jnp.where(column < key[to:to + 1], 1.0, 0.0)
            ranks[to] = ranks[to] + jnp.sum(less.reshape(LANES // 8, 8, LANES), axis=0)
    first_ref[...] = jnp.sum(first, axis=0, keepdims=True).astype(jnp.int32)
    copy = pltpu.make_async_copy(first_ref, first_hbm, sent)
    copy.start()
    first = jnp.sum(first, axis=0, keepdims=True)
    start = jnp.sum(jnp.where(iota((1, LANES), 1) == me_ref[0], first, 0.0), axis=1, keepdims=True).astype(jnp.int32)
    row, lane = iota((total // 2, LANES), 0), iota((total // 2, LANES), 1)
    row = row + jnp.where(lane < SLOTS, 0, total // 2)
    select = row - lax.bitwise_and(lane, SLOTS - 1) == start
    select_ref[...] = jnp.where(select, 1.0, 0.0).astype(BF16)
    spots = iota((total, LANES), 0)
    for to in range(rows):
        rank = jnp.sum(ranks[to], axis=0, keepdims=True).astype(jnp.int32)
        perm_ref[:, to * LANES:(to + 1) * LANES] = jnp.where(spots == rank, 1.0, 0.0).astype(BF16)

    source = source_ref[...]
    terms = [term.astype(F32) for term in three_terms(source)]
    product = source[0:1] * source[3:4] + source[1:2] * source[4:5] + source[2:3] * source[5:6]
    product = [term.astype(F32) for term in three_terms(product)]
    one = jnp.ones((3, count), F32)
    last = jnp.concatenate(product + [one, jnp.zeros((2, count), F32)], axis=0)
    stack = jnp.concatenate([terms[a] for a, unused in PAIRS] + [last], axis=0)
    mass = source[6:7]
    moments = jnp.concatenate([mass * source[0:6], mass, jnp.zeros((1, count), F32)], axis=0)
    moments = [term.astype(F32) for term in three_terms(moments)]
    moment_ref[...] = jnp.concatenate(moments + [jnp.zeros((8, count), F32)], axis=0).astype(BF16)
    for piece in range(count // LANES):
        here = slice(piece * LANES, (piece + 1) * LANES)
        across = jnp.transpose(stack[:, here])
        factor_ref[here, :] = jnp.concatenate([across, jnp.zeros((LANES, LANES - 56), F32)], axis=1).astype(BF16)
    copy.wait()


def prepare(me, source, active):
    count = source.shape[1]
    total = active.shape[0] * LANES
    return pl.pallas_call(
        prepare_kernel,
        out_shape=(
            jax.ShapeDtypeStruct((1, LANES), jnp.int32),
            jax.ShapeDtypeStruct((count, LANES), BF16),
            jax.ShapeDtypeStruct((32, count), BF16),
            jax.ShapeDtypeStruct((total, total), BF16),
            jax.ShapeDtypeStruct((total // 2, LANES), BF16),
        ),
        in_specs=[smem()] + [vmem()] * 2,
        out_specs=(hbm(),) + (vmem(),) * 4,
        scratch_shapes=[pltpu.VMEM((1, LANES), jnp.int32), pltpu.SemaphoreType.DMA],
        compiler_params=params(12),
        cost_estimate=cost(5),
        name="prepare",
    )(me, source, active)


def place(first_ref, states_ref, compact, half, owner):
    start = first_ref[0, owner]
    block = lax.shift_right_logical(start, 7)
    shift = lax.bitwise_and(start, LANES - 1)
    depth = states_ref.shape[0] // ROWS // PLANE_SIZE
    low = (owner % PLANE_SIZE * depth + owner // PLANE_SIZE) * ROWS
    if low + 8 <= states_ref.shape[0]:
        value = states_ref[low:low + 8]
    else:
        value = jnp.concatenate([states_ref[low:low + ROWS], jnp.zeros((8 - ROWS, LANES), F32)], axis=0)
    turned = pltpu.roll(value, lax.bitwise_and(shift + half * SLOTS, LANES - 1), 1)
    pltpu.store(compact.at[block], turned, mask=iota((8, LANES), 1) >= shift)
    compact[block + 1] = turned


def force_kernel(first_hbm, states_ref, factor_ref, moment_ref, send_ref, state_ref,
                 compact, later, first_ref, spread_ref, arrived):
    owners = states_ref.shape[0] // ROWS
    count = factor_ref.shape[0]
    blocks = send_ref.shape[1] // 6
    copy = pltpu.make_async_copy(first_hbm, first_ref, arrived)
    copy.start()
    row, column = iota((LANES, 3 * LANES), 0), iota((LANES, 3 * LANES), 1)
    coordinate = lax.shift_right_logical(column, 7)
    gather = (row == coordinate) | (row == coordinate + 16) | (row == coordinate + 40)
    gather = jnp.where(gather, 1.0, 0.0).astype(BF16)

    def spread(low, size):
        here = pl.ds(low, size)
        wide = jnp.dot(factor_ref[here, :], gather, preferred_element_type=F32)
        for d in range(3):
            spread_ref[d, here, :] = wide[:, d * LANES:(d + 1) * LANES]

    wide, deep = 2, min(1024, count)
    spread(0, deep)
    copy.wait()

    for owner in range(owners):
        place(first_ref, states_ref, compact, 0, owner)
    width = wide * LANES

    def part(block):
        tiles = [compact[block + b] for b in range(wide)]
        star = jnp.concatenate(tiles, axis=1)
        x, v = star[0:3], star[3:6]
        swapped = jnp.concatenate([-v, -x, jnp.zeros((2, width), F32)], axis=0)
        terms = [term.astype(F32) for term in three_terms(swapped)]
        product = [term.astype(F32) for term in three_terms(x[0:1] * v[0:1] + x[1:2] * v[1:2] + x[2:3] * v[2:3])]
        last = jnp.concatenate([jnp.ones((3, width), F32)] + product + [jnp.zeros((2, width), F32)], axis=0)
        cross = jnp.concatenate(
            [terms[b] for unused, b in PAIRS] + [last, jnp.zeros((LANES - 56, width), F32)], axis=0
        ).astype(BF16)
        weighted = jnp.zeros((32, width), F32)
        radial = jnp.zeros((32, width), F32)
        for low in range(0, count, deep):
            here = slice(low, low + deep)
            if block == 0 and low > 0:
                spread(low, deep)
            rel = [jnp.concatenate([spread_ref[d, here, :]] * wide, axis=1) - x[d:d + 1] for d in range(3)]
            dist = rel[0] * rel[0] + rel[1] * rel[1] + (rel[2] * rel[2] + softening)
            inv = lax.rsqrt(dist)
            inv2 = inv * inv
            weight = inv * inv2
            dot = jnp.dot(factor_ref[here, :], cross, preferred_element_type=F32)
            turn = weight * inv2 * dot
            moment = moment_ref[:, here]
            weight_high, turn_high = weight.astype(BF16), turn.astype(BF16)
            weight_low = (weight - weight_high.astype(F32)).astype(BF16)
            turn_low = (turn - turn_high.astype(F32)).astype(BF16)
            weighted = weighted + jnp.dot(moment, weight_high, preferred_element_type=F32)
            weighted = weighted + jnp.dot(moment, weight_low, preferred_element_type=F32)
            radial = radial + jnp.dot(moment, turn_high, preferred_element_type=F32)
            radial = radial + jnp.dot(moment, turn_low, preferred_element_type=F32)
        weighted = weighted[0:8] + weighted[8:16] + weighted[16:24]
        radial = radial[0:8] + radial[8:16] + radial[16:24]
        acc = weighted[0:3] - x * weighted[6:7]
        jrk = weighted[3:6] - v * weighted[6:7] - 3.0 * (radial[0:3] - x * radial[6:7])
        for b in range(wide):
            for d in range(3):
                send_ref[0, pl.ds(d * blocks + block + b, 1), :] = acc[d:d + 1, b * LANES:(b + 1) * LANES]
                send_ref[0, pl.ds((3 + d) * blocks + block + b, 1), :] = jrk[d:d + 1, b * LANES:(b + 1) * LANES]

    for step, block in enumerate(range(0, blocks, wide)):
        part(block)
        share = owners * wide // blocks
        for owner in range(step * share, (step + 1) * share):
            place(first_ref, states_ref, later, 1, owner)
    for field in range(8):
        state_ref[field] = later[0:blocks, field, :]
    for peer in range(1, send_ref.shape[0]):
        send_ref[peer] = send_ref[0]


def forces(first, states, factor, moment, blocks, peers):
    return pl.pallas_call(
        force_kernel,
        out_shape=(
            jax.ShapeDtypeStruct((peers, 6 * blocks, LANES), F32),
            jax.ShapeDtypeStruct((8, blocks, LANES), F32),
        ),
        in_specs=[hbm(), vmem(), vmem(), vmem()],
        out_specs=(vmem(), vmem()),
        scratch_shapes=[
            pltpu.VMEM((blocks + 2, 8, LANES), F32),
            pltpu.VMEM((blocks + 2, 8, LANES), F32),
            pltpu.SMEM(first.shape, first.dtype),
            pltpu.VMEM((3, factor.shape[0], LANES), F32),
            pltpu.SemaphoreType.DMA,
        ],
        compiler_params=params(12),
        cost_estimate=cost(9),
        name="forces",
    )(pinned(first), states, factor, moment)


def repeat_kernel(value_ref, send_ref):
    for low in range(0, value_ref.shape[0], 8):
        value = value_ref[low:low + 8]
        for peer in range(send_ref.shape[0]):
            send_ref[peer, low:low + 8, :] = value


def repeat(value, peers):
    return pl.pallas_call(
        repeat_kernel,
        out_shape=jax.ShapeDtypeStruct((peers,) + value.shape, F32),
        in_specs=[vmem()],
        out_specs=vmem(),
        compiler_params=params(4),
        name="repeat",
    )(value)


def add_rows(parts_ref, rows):
    parts = [parts_ref[part, rows, :] for part in range(parts_ref.shape[0])]
    while len(parts) > 1:
        parts = [one + two for one, two in zip(parts[0::2], parts[1::2])]
    return parts[0]


def add_kernel(parts_ref, send_ref):
    for low in range(0, parts_ref.shape[1], 8):
        rows = slice(low, low + 8)
        total = add_rows(parts_ref, rows)
        for peer in range(send_ref.shape[0]):
            send_ref[peer, rows, :] = total


def add_parts(parts, peers):
    return pl.pallas_call(
        add_kernel,
        out_shape=jax.ShapeDtypeStruct((peers,) + parts.shape[1:], F32),
        in_specs=[vmem()],
        out_specs=vmem(),
        compiler_params=params(4),
        name="add_parts",
    )(parts)


def correct_kernel(parts_ref, state_ref, select_ref, own_ref, terms_ref, wide):
    blocks = state_ref.shape[1]
    tau = state_ref[6]
    t2 = tau * tau
    for d in range(3):
        acc = add_rows(parts_ref, slice(d * blocks, (d + 1) * blocks))
        jrk = add_rows(parts_ref, slice((3 + d) * blocks, (4 + d) * blocks))
        wide[d] = state_ref[d] + t2 * (0.15 * acc - tau * (jrk / 30.0))
        wide[3 + d] = state_ref[3 + d] + tau * (0.5 * acc - tau * (jrk / 12.0))
        wide[6 + d] = acc
        wide[9 + d] = jrk
    for f in range(12, 16):
        wide[f] = jnp.ones_like(tau)
    value = jnp.concatenate([wide[:, block, :] for block in range(blocks)], axis=1)
    terms = jnp.concatenate(three_terms(value), axis=0)
    terms_ref[...] = terms
    half = select_ref.shape[0]
    low = jnp.dot(terms[:, 0:half], select_ref[...], preferred_element_type=F32)
    high = jnp.dot(terms[:, half:2 * half], select_ref[...], preferred_element_type=F32)
    low = low[0:16] + low[16:32] + low[32:48]
    high = high[0:16] + high[16:32] + high[32:48]
    own_ref[...] = low + pltpu.roll(high, SLOTS, 1)


def correct(parts, state, select):
    blocks = state.shape[1]
    return pl.pallas_call(
        correct_kernel,
        out_shape=(
            jax.ShapeDtypeStruct((16, LANES), F32),
            jax.ShapeDtypeStruct((48, blocks * LANES), BF16),
        ),
        in_specs=[vmem()] * 3,
        out_specs=(vmem(), vmem()),
        scratch_shapes=[pltpu.VMEM((16, blocks, LANES), F32)],
        compiler_params=params(4),
        name="correct",
    )(parts, state, select)


def permute_kernel(terms_ref, perm_ref, update_ref):
    result = jnp.dot(terms_ref[...], perm_ref[...], preferred_element_type=F32)
    update_ref[...] = (result[0:16] + result[16:32] + result[32:48])[0:12]


def permute(terms, perm):
    return pl.pallas_call(
        permute_kernel,
        out_shape=jax.ShapeDtypeStruct((12, perm.shape[1]), F32),
        in_specs=[vmem(), vmem()],
        out_specs=vmem(),
        compiler_params=params(8),
        cost_estimate=cost(2),
        name="permute",
    )(terms, perm)


def write_kernel(mine_ref, other_ref, here_ref, there_ref, pos_ref, vel_ref, acc_ref, jrk_ref,
                 new_pos_ref, new_vel_ref, new_acc_ref, new_jrk_ref):
    count = pos_ref.shape[1]
    both = jnp.concatenate([mine_ref[:, 0:SLOTS], other_ref[:, 0:SLOTS]], axis=1)
    place = jnp.concatenate([here_ref[...], there_ref[...]], axis=0)[:, 0:1]
    onehot = jnp.where(iota((2 * SLOTS, count), 1) == place, 1.0, 0.0).astype(BF16)
    values = jnp.dot(jnp.concatenate(three_terms(both), axis=0), onehot, preferred_element_type=F32)
    values = values[0:16] + values[16:32] + values[32:48]
    hit = values[12:13] > 0.5
    new_pos_ref[...] = jnp.where(hit, values[0:3], pos_ref[...])
    new_vel_ref[...] = jnp.where(hit, values[3:6], vel_ref[...])
    new_acc_ref[...] = jnp.where(hit, values[6:9], acc_ref[...])
    new_jrk_ref[...] = jnp.where(hit, values[9:12], jrk_ref[...])


def write(mine, other, here, there, position, velocity, accel, jerk_old):
    shape = jax.ShapeDtypeStruct(position.shape, F32)
    return pl.pallas_call(
        write_kernel,
        out_shape=(shape,) * 4,
        in_specs=[vmem()] * 8,
        out_specs=(vmem(),) * 4,
        compiler_params=params(4),
        name="write",
    )(mine, other, here, there, position, velocity, accel, jerk_old)


def swap(value):
    return lax.ppermute(value, "core", [(0, 1), (1, 0)])


def exchange(value, axes):
    return lax.all_to_all(value, axes, 0, 0, tiled=True)


def local(owners, plane, depth, position, velocity, accel, jerk_old, masses, phase, levels, active):
    count = position.shape[1]
    blocks = active.shape[0]
    me = lax.axis_index(SRC).reshape(1).astype(jnp.int32)
    send, source, mine = pick(
        me, position, velocity, accel, jerk_old, masses.reshape(1, count), phase.reshape(1, count),
        levels.reshape(1, count), active, depth,
    )
    column = exchange(send.reshape(depth, ROWS, 1, LANES), "z").reshape(send.shape)
    column, late, mine = lax.optimization_barrier((column, active, mine))
    states = exchange(repeat(column, plane), PLANE).reshape(owners * ROWS, LANES)
    other = swap(mine)
    first, factor, moment, perm, select = prepare(me, source, late)
    states, other, perm, select = lax.optimization_barrier((states, other, perm, select))
    send, state = forces(first, states, factor, moment, blocks, plane)
    parts = exchange(add_parts(exchange(send, PLANE), depth), "z")
    own, terms = correct(parts, state, select)
    update = permute(terms, perm)
    new = write(own, swap(own), mine, other, position, velocity, accel, jerk_old)
    return new + (update,)


def solution(mesh):
    owners = mesh.shape["src"]
    plane = PLANE_SIZE
    depth = owners // plane
    fine = Mesh(mesh.devices.reshape(depth, 4, 4, mesh.shape["act"]), ("z", "y", "x", "core"))
    stars = P(None, SRC)
    placed = (stars,) * 4 + (P(SRC),) * 3 + (P("core", None),)
    return jax.shard_map(
        lambda *arrays: local(owners, plane, depth, *arrays),
        mesh=fine,
        in_specs=placed,
        out_specs=(stars,) * 4 + (P(None, "core"),),
        check_vma=False,
    )
```

```python
import jax
import jax.numpy as jnp
from jax import lax
from jax.experimental import pallas as pl
from jax.experimental.pallas import tpu as pltpu
from jax.sharding import Mesh
from jax.sharding import PartitionSpec as P

softening = 0.0025
SLOTS = 64
ROWS = 7
LANES = 128
PLANE = ("y", "x")
PLANE_SIZE = 16
SRC = ("z", "y", "x")
F32 = jnp.float32
BF16 = jnp.bfloat16
PREP = 12
PAIRS = ((0, 0), (0, 1), (1, 0), (1, 1), (0, 2), (2, 0))


def params(mebibytes):
    return pltpu.CompilerParams(vmem_limit_bytes=mebibytes << 20)


def cost(microseconds):
    return pl.CostEstimate(flops=0, transcendentals=0, bytes_accessed=microseconds * 3000000)


def vmem():
    return pl.BlockSpec(memory_space=pltpu.VMEM)


def hbm():
    return pl.BlockSpec(memory_space=pltpu.HBM)


def pinned(value):
    return pltpu.with_memory_space_constraint(value, pltpu.HBM)


def smem():
    return pl.BlockSpec(memory_space=pltpu.SMEM)


def three_terms(value):
    high = value.astype(BF16)
    rest = value - high.astype(F32)
    middle = rest.astype(BF16)
    low = (rest - middle.astype(F32)).astype(BF16)
    return high, middle, low


def iota(shape, axis):
    return lax.broadcasted_iota(jnp.int32, shape, axis)


def pick_kernel(active_hbm, *refs):
    inputs, send_ref, source_ref, place_ref = refs[0:7], refs[7], refs[8], refs[9]
    active_ref, kept, arrived = refs[10], refs[11:18], refs[18]
    copies = [pltpu.make_async_copy(active_hbm, active_ref, arrived.at[7])]
    copies += [pltpu.make_async_copy(here, there, arrived.at[i]) for i, (here, there) in enumerate(zip(inputs, kept))]
    for copy in copies:
        copy.start()
    count = kept[0].shape[1]
    rows = active_ref.shape[0]
    copies[0].wait()
    offset = active_ref[...] - lax.axis_index(SRC) * count
    owned = (offset >= 0) & (offset < count)
    flag = jnp.where(owned, 1.0, 0.0)
    before = jnp.where(iota((LANES, LANES), 0) < iota((LANES, LANES), 1), 1.0, 0.0)
    inside = jnp.dot(flag.astype(BF16), before.astype(BF16), preferred_element_type=F32)
    totals = jnp.sum(flag, axis=1, keepdims=True)
    running = jnp.zeros((1, 1), F32)
    place = jnp.zeros((SLOTS, LANES), jnp.int32)
    slot_id = iota((SLOTS, LANES), 0)
    for row in range(rows):
        slot = (inside[row:row + 1] + running).astype(jnp.int32)
        slot = jnp.where(owned[row:row + 1], slot, -1)
        place = place + jnp.where(slot_id == slot, offset[row:row + 1] + 1, 0)
        running = running + totals[row:row + 1]
    spot = jnp.sum(place.astype(F32), axis=1, keepdims=True).astype(jnp.int32) - 1
    place_ref[...] = jnp.broadcast_to(spot, (SLOTS, LANES))
    onehot = jnp.where(iota((SLOTS, count), 1) == spot, 1.0, 0.0).astype(BF16)

    for copy in copies[1:]:
        copy.wait()
    position, velocity, accel, jerk, mass, phase, level = [ref[...] for ref in kept]
    tau = phase * jnp.exp2(-level.astype(F32))
    pred_x = position + tau * (velocity + tau * (accel * 0.5 + tau * (jerk / 6.0)))
    pred_v = velocity + tau * (accel + tau * (jerk * 0.5))
    base_x = pred_x - tau * tau * (0.15 * accel + tau * (jerk * (7.0 / 60.0)))
    base_v = pred_v - tau * (0.5 * accel + tau * (jerk * (5.0 / 12.0)))
    source_ref[...] = jnp.concatenate([pred_x, pred_v, mass, tau], axis=0)
    table = jnp.concatenate([pred_x, pred_v, tau, tau, base_x, base_v, tau, tau], axis=0)
    terms = jnp.concatenate(three_terms(table), axis=0)
    picked = lax.dot_general(terms, onehot, (((1,), (1,)), ((), ())), preferred_element_type=F32)
    picked = picked[0:16] + picked[16:32] + picked[32:48]
    block = jnp.concatenate([picked[0:8], picked[8:16]], axis=1)[0:ROWS]
    blocks = jnp.concatenate([block] * (send_ref.shape[0] // ROWS), axis=0)
    send_ref[...] = blocks


def pick(position, velocity, accel, jerk_old, masses, phase, levels, active, peers):
    count = position.shape[1]
    inputs = (position, velocity, accel, jerk_old, masses, phase, levels)
    return pl.pallas_call(
        pick_kernel,
        out_shape=(
            jax.ShapeDtypeStruct((peers * ROWS, LANES), F32),
            jax.ShapeDtypeStruct((8, count), F32),
            jax.ShapeDtypeStruct((SLOTS, LANES), jnp.int32),
        ),
        in_specs=[hbm()] * 8,
        out_specs=(vmem(), vmem(), vmem()),
        scratch_shapes=[pltpu.VMEM(value.shape, value.dtype) for value in (active,) + inputs]
        + [pltpu.SemaphoreType.DMA((8,))],
        compiler_params=params(8),
        name="pick",
    )(pinned(active), *[pinned(value) for value in inputs])


def sort_keys(active, count):
    rows = active.shape[0]
    owner = lax.shift_right_logical(active, count.bit_length() - 1)
    return (owner * (rows * LANES) + iota((rows, LANES), 0) * LANES + iota((rows, LANES), 1)).astype(F32)


def prepare_kernel(me_ref, source_ref, active_ref, first_hbm, factor_ref, moment_ref, perm_ref, select_ref,
                   first_ref, sent):
    count = source_ref.shape[1]
    rows = active_ref.shape[0]
    total = rows * LANES
    key = sort_keys(active_ref[...], count)
    columns = jnp.transpose(key)
    limit = (iota((1, LANES), 1) * total).astype(F32)
    first = jnp.zeros((8, LANES), F32)
    ranks = [jnp.zeros((8, LANES), F32) for _ in range(rows)]
    for row in range(rows):
        column = jnp.broadcast_to(columns[:, row:row + 1], (LANES, LANES))
        first = first + jnp.sum(jnp.where(column < limit, 1.0, 0.0).reshape(LANES // 8, 8, LANES), axis=0)
        for to in range(rows):
            less = jnp.where(column < key[to:to + 1], 1.0, 0.0)
            ranks[to] = ranks[to] + jnp.sum(less.reshape(LANES // 8, 8, LANES), axis=0)
    first_ref[...] = jnp.sum(first, axis=0, keepdims=True).astype(jnp.int32)
    copy = pltpu.make_async_copy(first_ref, first_hbm, sent)
    copy.start()
    first = jnp.sum(first, axis=0, keepdims=True)
    start = jnp.sum(jnp.where(iota((1, LANES), 1) == me_ref[0], first, 0.0), axis=1, keepdims=True).astype(jnp.int32)
    row, lane = iota((total // 2, LANES), 0), iota((total // 2, LANES), 1)
    row = row + jnp.where(lane < SLOTS, 0, total // 2)
    select = row - lax.bitwise_and(lane, SLOTS - 1) == start
    select_ref[...] = jnp.where(select, 1.0, 0.0).astype(BF16)
    spots = iota((total, LANES), 0)
    for to in range(rows):
        rank = jnp.sum(ranks[to], axis=0, keepdims=True).astype(jnp.int32)
        perm_ref[:, to * LANES:(to + 1) * LANES] = jnp.where(spots == rank, 1.0, 0.0).astype(BF16)

    source = source_ref[...]
    terms = [term.astype(F32) for term in three_terms(source)]
    product = source[0:1] * source[3:4] + source[1:2] * source[4:5] + source[2:3] * source[5:6]
    product = [term.astype(F32) for term in three_terms(product)]
    one = jnp.ones((3, count), F32)
    last = jnp.concatenate(product + [one, jnp.zeros((2, count), F32)], axis=0)
    stack = jnp.concatenate([terms[a] for a, unused in PAIRS] + [last], axis=0)
    mass = source[6:7]
    moments = jnp.concatenate([mass * source[0:6], mass, jnp.zeros((1, count), F32)], axis=0)
    moments = [term.astype(F32) for term in three_terms(moments)]
    moment_ref[...] = jnp.concatenate(moments + [jnp.zeros((8, count), F32)], axis=0).astype(BF16)
    for piece in range(count // LANES):
        here = slice(piece * LANES, (piece + 1) * LANES)
        across = jnp.transpose(stack[:, here])
        factor_ref[here, :] = jnp.concatenate([across, jnp.zeros((LANES, LANES - 56), F32)], axis=1).astype(BF16)
    copy.wait()


def prepare(me, source, active):
    count = source.shape[1]
    total = active.shape[0] * LANES
    return pl.pallas_call(
        prepare_kernel,
        out_shape=(
            jax.ShapeDtypeStruct((1, LANES), jnp.int32),
            jax.ShapeDtypeStruct((count, LANES), BF16),
            jax.ShapeDtypeStruct((32, count), BF16),
            jax.ShapeDtypeStruct((total, total), BF16),
            jax.ShapeDtypeStruct((total // 2, LANES), BF16),
        ),
        in_specs=[smem()] + [vmem()] * 2,
        out_specs=(hbm(),) + (vmem(),) * 4,
        scratch_shapes=[pltpu.VMEM((1, LANES), jnp.int32), pltpu.SemaphoreType.DMA],
        compiler_params=params(12),
        cost_estimate=cost(5),
        name="prepare",
    )(me, source, active)


def place(first_ref, states_ref, compact, half, owner):
    start = first_ref[0, owner]
    block = lax.shift_right_logical(start, 7)
    shift = lax.bitwise_and(start, LANES - 1)
    depth = states_ref.shape[0] // ROWS // PLANE_SIZE
    low = (owner % PLANE_SIZE * depth + owner // PLANE_SIZE) * ROWS
    if low + 8 <= states_ref.shape[0]:
        value = states_ref[low:low + 8]
    else:
        value = jnp.concatenate([states_ref[low:low + ROWS], jnp.zeros((8 - ROWS, LANES), F32)], axis=0)
    turned = pltpu.roll(value, lax.bitwise_and(shift + half * SLOTS, LANES - 1), 1)
    pltpu.store(compact.at[block], turned, mask=iota((8, LANES), 1) >= shift)
    compact[block + 1] = turned


def force_kernel(first_hbm, states_ref, factor_ref, moment_ref, send_ref, state_ref,
                 compact, later, first_ref, spread_ref, arrived):
    owners = states_ref.shape[0] // ROWS
    count = factor_ref.shape[0]
    blocks = send_ref.shape[1] // 6
    copy = pltpu.make_async_copy(first_hbm, first_ref, arrived)
    copy.start()
    row, column = iota((LANES, 3 * LANES), 0), iota((LANES, 3 * LANES), 1)
    coordinate = lax.shift_right_logical(column, 7)
    gather = (row == coordinate) | (row == coordinate + 16) | (row == coordinate + 40)
    gather = jnp.where(gather, 1.0, 0.0).astype(BF16)

    def spread(low, size):
        here = pl.ds(low, size)
        wide = jnp.dot(factor_ref[here, :], gather, preferred_element_type=F32)
        for d in range(3):
            spread_ref[d, here, :] = wide[:, d * LANES:(d + 1) * LANES]

    wide, deep = 2, min(1024, count)
    spread(0, deep)
    copy.wait()

    for owner in range(owners):
        place(first_ref, states_ref, compact, 0, owner)
    width = wide * LANES

    def part(block):
        tiles = [compact[block + b] for b in range(wide)]
        star = jnp.concatenate(tiles, axis=1)
        x, v = star[0:3], star[3:6]
        swapped = jnp.concatenate([-v, -x, jnp.zeros((2, width), F32)], axis=0)
        terms = [term.astype(F32) for term in three_terms(swapped)]
        product = [term.astype(F32) for term in three_terms(x[0:1] * v[0:1] + x[1:2] * v[1:2] + x[2:3] * v[2:3])]
        last = jnp.concatenate([jnp.ones((3, width), F32)] + product + [jnp.zeros((2, width), F32)], axis=0)
        cross = jnp.concatenate(
            [terms[b] for unused, b in PAIRS] + [last, jnp.zeros((LANES - 56, width), F32)], axis=0
        ).astype(BF16)
        weighted = jnp.zeros((32, width), F32)
        radial = jnp.zeros((32, width), F32)
        for low in range(0, count, deep):
            here = slice(low, low + deep)
            if block == 0 and low > 0:
                spread(low, deep)
            rel = [jnp.concatenate([spread_ref[d, here, :]] * wide, axis=1) - x[d:d + 1] for d in range(3)]
            dist = rel[0] * rel[0] + rel[1] * rel[1] + (rel[2] * rel[2] + softening)
            inv = lax.rsqrt(dist)
            inv2 = inv * inv
            weight = inv * inv2
            dot = jnp.dot(factor_ref[here, :], cross, preferred_element_type=F32)
            turn = weight * inv2 * dot
            moment = moment_ref[:, here]
            weight_high, turn_high = weight.astype(BF16), turn.astype(BF16)
            weight_low = (weight - weight_high.astype(F32)).astype(BF16)
            turn_low = (turn - turn_high.astype(F32)).astype(BF16)
            weighted = weighted + jnp.dot(moment, weight_high, preferred_element_type=F32)
            weighted = weighted + jnp.dot(moment, weight_low, preferred_element_type=F32)
            radial = radial + jnp.dot(moment, turn_high, preferred_element_type=F32)
            radial = radial + jnp.dot(moment, turn_low, preferred_element_type=F32)
        weighted = weighted[0:8] + weighted[8:16] + weighted[16:24]
        radial = radial[0:8] + radial[8:16] + radial[16:24]
        acc = weighted[0:3] - x * weighted[6:7]
        jrk = weighted[3:6] - v * weighted[6:7] - 3.0 * (radial[0:3] - x * radial[6:7])
        for b in range(wide):
            for d in range(3):
                send_ref[0, pl.ds(d * blocks + block + b, 1), :] = acc[d:d + 1, b * LANES:(b + 1) * LANES]
                send_ref[0, pl.ds((3 + d) * blocks + block + b, 1), :] = jrk[d:d + 1, b * LANES:(b + 1) * LANES]

    for step, block in enumerate(range(0, blocks, wide)):
        part(block)
        share = owners * wide // blocks
        for owner in range(step * share, (step + 1) * share):
            place(first_ref, states_ref, later, 1, owner)
    for field in range(8):
        state_ref[field] = later[0:blocks, field, :]
    for peer in range(1, send_ref.shape[0]):
        send_ref[peer] = send_ref[0]


def forces(first, states, factor, moment, blocks, peers):
    return pl.pallas_call(
        force_kernel,
        out_shape=(
            jax.ShapeDtypeStruct((peers, 6 * blocks, LANES), F32),
            jax.ShapeDtypeStruct((8, blocks, LANES), F32),
        ),
        in_specs=[hbm(), vmem(), vmem(), vmem()],
        out_specs=(vmem(), vmem()),
        scratch_shapes=[
            pltpu.VMEM((blocks + 2, 8, LANES), F32),
            pltpu.VMEM((blocks + 2, 8, LANES), F32),
            pltpu.SMEM(first.shape, first.dtype),
            pltpu.VMEM((3, factor.shape[0], LANES), F32),
            pltpu.SemaphoreType.DMA,
        ],
        compiler_params=params(12),
        cost_estimate=cost(9),
        name="forces",
    )(pinned(first), states, factor, moment)


def repeat_kernel(value_ref, send_hbm, sent):
    copies = [pltpu.make_async_copy(value_ref, send_hbm.at[peer], sent.at[peer]) for peer in range(send_hbm.shape[0])]
    for copy in copies:
        copy.start()
    for copy in copies:
        copy.wait()


def repeat(value, peers):
    return pl.pallas_call(
        repeat_kernel,
        out_shape=jax.ShapeDtypeStruct((peers,) + value.shape, F32),
        in_specs=[vmem()],
        out_specs=hbm(),
        scratch_shapes=[pltpu.SemaphoreType.DMA((peers,))],
        compiler_params=params(4),
        name="repeat",
    )(value)


def add_rows(parts_ref, rows):
    parts = [parts_ref[part, rows, :] for part in range(parts_ref.shape[0])]
    while len(parts) > 1:
        parts = [one + two for one, two in zip(parts[0::2], parts[1::2])]
    return parts[0]


def add_kernel(parts_ref, send_ref):
    for low in range(0, parts_ref.shape[1], 8):
        rows = slice(low, low + 8)
        total = add_rows(parts_ref, rows)
        for peer in range(send_ref.shape[0]):
            send_ref[peer, rows, :] = total


def add_parts(parts, peers):
    return pl.pallas_call(
        add_kernel,
        out_shape=jax.ShapeDtypeStruct((peers,) + parts.shape[1:], F32),
        in_specs=[vmem()],
        out_specs=vmem(),
        compiler_params=params(4),
        name="add_parts",
    )(parts)


def correct_kernel(parts_ref, state_ref, select_ref, own_ref, terms_ref, wide):
    blocks = state_ref.shape[1]
    tau = state_ref[6]
    t2 = tau * tau
    for d in range(3):
        acc = add_rows(parts_ref, slice(d * blocks, (d + 1) * blocks))
        jrk = add_rows(parts_ref, slice((3 + d) * blocks, (4 + d) * blocks))
        wide[d] = state_ref[d] + t2 * (0.15 * acc - tau * (jrk / 30.0))
        wide[3 + d] = state_ref[3 + d] + tau * (0.5 * acc - tau * (jrk / 12.0))
        wide[6 + d] = acc
        wide[9 + d] = jrk
    for f in range(12, 16):
        wide[f] = jnp.ones_like(tau)
    value = jnp.concatenate([wide[:, block, :] for block in range(blocks)], axis=1)
    terms = jnp.concatenate(three_terms(value), axis=0)
    terms_ref[...] = terms
    half = select_ref.shape[0]
    low = jnp.dot(terms[:, 0:half], select_ref[...], preferred_element_type=F32)
    high = jnp.dot(terms[:, half:2 * half], select_ref[...], preferred_element_type=F32)
    low = low[0:16] + low[16:32] + low[32:48]
    high = high[0:16] + high[16:32] + high[32:48]
    own_ref[...] = low + pltpu.roll(high, SLOTS, 1)


def correct(parts, state, select):
    blocks = state.shape[1]
    return pl.pallas_call(
        correct_kernel,
        out_shape=(
            jax.ShapeDtypeStruct((16, LANES), F32),
            jax.ShapeDtypeStruct((48, blocks * LANES), BF16),
        ),
        in_specs=[vmem()] * 3,
        out_specs=(vmem(), vmem()),
        scratch_shapes=[pltpu.VMEM((16, blocks, LANES), F32)],
        compiler_params=params(4),
        name="correct",
    )(parts, state, select)


def permute_kernel(terms_ref, perm_ref, update_ref):
    result = jnp.dot(terms_ref[...], perm_ref[...], preferred_element_type=F32)
    update_ref[...] = (result[0:16] + result[16:32] + result[32:48])[0:12]


def permute(terms, perm):
    return pl.pallas_call(
        permute_kernel,
        out_shape=jax.ShapeDtypeStruct((12, perm.shape[1]), F32),
        in_specs=[vmem(), vmem()],
        out_specs=vmem(),
        compiler_params=params(8),
        cost_estimate=cost(2),
        name="permute",
    )(terms, perm)


def write_kernel(mine_ref, other_ref, here_ref, there_ref, pos_ref, vel_ref, acc_ref, jrk_ref,
                 new_pos_ref, new_vel_ref, new_acc_ref, new_jrk_ref):
    count = pos_ref.shape[1]
    both = jnp.concatenate([mine_ref[:, 0:SLOTS], other_ref[:, 0:SLOTS]], axis=1)
    place = jnp.concatenate([here_ref[...], there_ref[...]], axis=0)[:, 0:1]
    onehot = jnp.where(iota((2 * SLOTS, count), 1) == place, 1.0, 0.0).astype(BF16)
    values = jnp.dot(jnp.concatenate(three_terms(both), axis=0), onehot, preferred_element_type=F32)
    values = values[0:16] + values[16:32] + values[32:48]
    hit = values[12:13] > 0.5
    new_pos_ref[...] = jnp.where(hit, values[0:3], pos_ref[...])
    new_vel_ref[...] = jnp.where(hit, values[3:6], vel_ref[...])
    new_acc_ref[...] = jnp.where(hit, values[6:9], acc_ref[...])
    new_jrk_ref[...] = jnp.where(hit, values[9:12], jrk_ref[...])


def write(mine, other, here, there, position, velocity, accel, jerk_old):
    shape = jax.ShapeDtypeStruct(position.shape, F32)
    return pl.pallas_call(
        write_kernel,
        out_shape=(shape,) * 4,
        in_specs=[vmem()] * 8,
        out_specs=(vmem(),) * 4,
        compiler_params=params(4),
        name="write",
    )(mine, other, here, there, position, velocity, accel, jerk_old)


def swap(value):
    return lax.ppermute(value, "core", [(0, 1), (1, 0)])


def exchange(value, axes):
    return lax.all_to_all(value, axes, 0, 0, tiled=True)


def local(owners, plane, depth, position, velocity, accel, jerk_old, masses, phase, levels, active):
    count = position.shape[1]
    blocks = active.shape[0]
    me = lax.axis_index(SRC).reshape(1).astype(jnp.int32)
    send, source, mine = pick(
        position, velocity, accel, jerk_old, masses.reshape(1, count), phase.reshape(1, count),
        levels.reshape(1, count), active, depth,
    )
    column = exchange(send.reshape(depth, ROWS, 1, LANES), "z").reshape(send.shape)
    column, late, mine = lax.optimization_barrier((column, active, mine))
    states = exchange(repeat(column, plane), PLANE).reshape(owners * ROWS, LANES)
    other = swap(mine)
    first, factor, moment, perm, select = prepare(me, source, late)
    states, other, perm, select = lax.optimization_barrier((states, other, perm, select))
    send, state = forces(first, states, factor, moment, blocks, plane)
    parts = exchange(add_parts(exchange(send, PLANE), depth), "z")
    own, terms = correct(parts, state, select)
    update = permute(terms, perm)
    new = write(own, swap(own), mine, other, position, velocity, accel, jerk_old)
    return new + (update,)


def solution(mesh):
    owners = mesh.shape["src"]
    plane = PLANE_SIZE
    depth = owners // plane
    fine = Mesh(mesh.devices.reshape(depth, 4, 4, mesh.shape["act"]), ("z", "y", "x", "core"))
    stars = P(None, SRC)
    placed = (stars,) * 4 + (P(SRC),) * 3 + (P("core", None),)
    return jax.shard_map(
        lambda *arrays: local(owners, plane, depth, *arrays),
        mesh=fine,
        in_specs=placed,
        out_specs=(stars,) * 4 + (P(None, "core"),),
        check_vma=False,
    )
```
